32 devices in a mesh: seq: 8 (over y, x, core), chan: 4 (over z).
Axes of the slice: x: 2, y: 2, z: 4, core: 2. Of those that a mesh axis runs over, the one named last changes fastest.
Arguments:
- latent: bfloat16 [4096, 16], P(('seq', 'chan')), may hold values from -140 to 140
- in_weight: bfloat16 [9, 16, 384], P(None, 'chan'), may hold values from -2 to 2
- in_bias: float32 [384], P('chan'), may hold values from -1.75 to 1.75
- norm_gain: float32 [3, 2, 384], P(None, None, 'chan'), may hold values from 0.1 to 1.9
- norm_shift: float32 [3, 2, 384], P(None, None, 'chan'), may hold values from -1.75 to 1.75
- res_weight: bfloat16 [3, 2, 9, 384, 384], P(None, None, None, 'chan'), may hold values from -2 to 2
- res_bias: float32 [3, 2, 384], P(None, None, 'chan'), may hold values from -1.75 to 1.75
- up_weight: bfloat16 [9, 384, 192], P(None, 'chan'), may hold values from -0.109375 to 0.109375
- up_bias: float32 [192], P('chan'), may hold values from -1.75 to 1.75
Outputs:
- image: bfloat16 [192, 32, 512], P('chan', 'seq')
The draws below stay inside these ranges and needn't reach their ends.
All inputs are finite; a program needn't handle non-finite values.
Results may differ from the reference program's by a relative error of at most 0.022.
Values may be sent and summed in bfloat16 or wider, within the bound.
No kernel may reach another device: no remote copies, remote signals or barrier semaphores. Data moves between devices by JAX's collectives and lax.ppermute only.
A program may use at most 64 MiB of HBM per device.

```python
import math
import jax
import jax.numpy as jnp
from jax import lax

LAT_C = 16
CH = 384
UP_CH = 192
LAYERS = 3
LAT_W = 256
HEIGHT = 16
TOKENS = 4096
N_CHAN = 4


def draw_latent(key, part):
    noise_key, token_key, chan_key = jax.random.split(key, 3)
    row_index = (jnp.arange(TOKENS, dtype=jnp.int32) // LAT_W).astype(jnp.float32)
    height_pos = row_index / max(HEIGHT - 1, 1)
    token_scale = jnp.exp(jax.random.uniform(token_key, (TOKENS,), jnp.float32, math.log(0.3), math.log(3.0)))
    chan_scale = jnp.exp(jax.random.uniform(chan_key, (LAT_C,), jnp.float32, math.log(0.5), math.log(2.0)))
    ramp = jnp.exp(math.log(3.0) * height_pos)
    base = jax.random.truncated_normal(noise_key, -4.0, 4.0, (TOKENS, LAT_C), jnp.float32)
    values = base * token_scale[:, None] * chan_scale[None, :] * ramp[:, None]
    return values.astype(jnp.bfloat16)


def rising_weight(key, shape, fan_in):
    noise_key, factor_key = jax.random.split(key, 2)
    outputs = shape[-1]
    position = jnp.arange(outputs, dtype=jnp.int32).astype(jnp.float32) / max(outputs - 1, 1)
    factor = jnp.exp(jax.random.uniform(factor_key, (outputs,), jnp.float32, math.log(0.7), math.log(1.4)))
    ramp = jnp.exp(math.log(8.0) * (position - 0.5))
    base = jax.random.truncated_normal(noise_key, -4.0, 4.0, shape, jnp.float32)
    return base * (ramp * factor) * fan_in ** (-0.5)


def draw_in_weight(key, part):
    values = rising_weight(jax.random.fold_in(key, 11), (9, LAT_C, CH), 9.0 * LAT_C)
    return values.astype(jnp.bfloat16)


def draw_res_weight(key, part):
    values = rising_weight(jax.random.fold_in(key, 23), (LAYERS, 2, 9, CH, CH), 9.0 * CH)
    return values.astype(jnp.bfloat16)


def block_levels(key, extent, cuts, least, high):
    loudness = 1.0
    for axis_at, parts in cuts:
        heights = jax.random.uniform(jax.random.fold_in(jax.random.fold_in(key, 6), axis_at), (parts,), jnp.float32, least / len(cuts), high / len(cuts))
        loudness = loudness * jnp.repeat(jnp.exp(heights), extent[axis_at] // parts).reshape((-1,) + (1,) * (len(extent) - 1 - axis_at))
    return loudness


def scatter_about(stream_key, shape, spread, limit, cuts=(), kind=jnp.bfloat16):
    array = jax.random.normal(stream_key, shape, jnp.float32) * spread
    if len(cuts) > 0:
        array = block_levels(stream_key, shape, cuts, -0.22, 0.18) * array
    return jnp.clip(array, min=-limit, max=limit).astype(kind)


def setup_inputs(seed: int = 0) -> dict:
    streams_of = jax.random.split(jax.random.key(seed), 10)
    latent = draw_latent(jax.random.fold_in(streams_of[9], 71), 0)
    in_weight = draw_in_weight(jax.random.fold_in(streams_of[9], 71), 0)
    in_bias = scatter_about(streams_of[2], (CH,), 0.3, 1.75, ((0, 4),), jnp.float32)
    norm_gain = jnp.clip(1.0 + 0.18 * jax.random.normal(streams_of[3], (LAYERS, 2, CH), jnp.float32), 0.1, 1.9)
    norm_shift = scatter_about(streams_of[4], (LAYERS, 2, CH), 0.3, 1.75, ((2, 4),), jnp.float32)
    res_weight = draw_res_weight(jax.random.fold_in(streams_of[9], 71), 0)
    res_bias = scatter_about(streams_of[6], (LAYERS, 2, CH), 0.3, 1.75, ((2, 4),), jnp.float32)
    up_weight = scatter_about(streams_of[7], (9, CH, UP_CH), (9 * CH) ** -0.5, 0.109375, ((1, 4),))
    up_bias = scatter_about(streams_of[8], (UP_CH,), 0.3, 1.75, ((0, 4),), jnp.float32)
    return dict(latent=latent, in_weight=in_weight, in_bias=in_bias, norm_gain=norm_gain, norm_shift=norm_shift, res_weight=res_weight, res_bias=res_bias, up_weight=up_weight, up_bias=up_bias)


EPS = 1e-06

def conv_sum(values, weight, bias):
    chans, height, width = values.shape
    outputs = weight.shape[2]
    quarter = chans // N_CHAN
    padded = jnp.pad(values, ((0, 0), (1, 1), (1, 1)))

    def quarter_sum(index):
        block = lax.dynamic_slice_in_dim(padded, index * quarter, quarter, 0).astype(jnp.float32)
        taps = lax.dynamic_slice_in_dim(weight, index * quarter, quarter, 1).astype(jnp.float32)
        totals = jnp.zeros((outputs, height * width), jnp.float32)
        for tap_index in range(9):
            row_off = tap_index // 3
            col_off = tap_index % 3
            window = block[:, row_off:row_off + height, col_off:col_off + width].reshape(quarter, height * width)
            totals = totals + jnp.dot(taps[tap_index].T, window, preferred_element_type=jnp.float32)
        return totals.astype(jnp.bfloat16)
    pieces = lax.map(quarter_sum, jnp.arange(N_CHAN, dtype=jnp.int32))
    summed = lax.optimization_barrier(jnp.sum(pieces.astype(jnp.float32), axis=0)) + bias[:, None]
    return summed.reshape(outputs, height, width)

def rms_norm(values, gain_vec, shift_vec):
    mean_sq = lax.optimization_barrier(jnp.mean(values * values, axis=0, keepdims=True))
    normed = values * lax.rsqrt(mean_sq + EPS)
    return normed * gain_vec[:, None, None] + shift_vec[:, None, None]

def reference(latent, in_weight, in_bias, norm_gain, norm_shift, res_weight, res_bias, up_weight, up_bias):
    slab_field = latent.T.reshape(LAT_C, HEIGHT, LAT_W)
    stream = conv_sum(slab_field, in_weight, in_bias).astype(jnp.bfloat16)
    for layer_idx in range(LAYERS):
        normed = jax.nn.silu(rms_norm(stream.astype(jnp.float32), norm_gain[layer_idx, 0], norm_shift[layer_idx, 0])).astype(jnp.bfloat16)
        middle = conv_sum(normed, res_weight[layer_idx, 0], res_bias[layer_idx, 0])
        branch_in = jax.nn.silu(rms_norm(middle, norm_gain[layer_idx, 1], norm_shift[layer_idx, 1])).astype(jnp.bfloat16)
        stream = (stream.astype(jnp.float32) + conv_sum(branch_in, res_weight[layer_idx, 1], res_bias[layer_idx, 1])).astype(jnp.bfloat16)
    widened = jnp.repeat(jnp.repeat(stream, 2, axis=1), 2, axis=2)
    return conv_sum(widened, up_weight, up_bias).astype(jnp.bfloat16)
```

```python
import functools
import jax
import jax.numpy as jnp
from jax import lax
from jax.experimental import pallas as pl
from jax.experimental.pallas import tpu as pltpu
from jax.sharding import PartitionSpec as P

LAT_W = 256
EPS = 1e-06
HALO = 8
VMEM_BYTES = 48 * 1024 * 1024

CORE, NEAR, FAR = 1, 2, 4


def place():
    seq = lax.axis_index("seq")
    return lax.rem(seq, 2), lax.rem(lax.div(seq, 2), 4)


def swap(array, mask):
    seqs, chans = lax.axis_size("seq"), lax.axis_size("chan")
    pairs = [(s * chans + c, (s ^ mask) * chans + c) for s in range(seqs) for c in range(chans)]
    return lax.ppermute(array, ("seq", "chan"), pairs)


def shift(array):
    seqs, chans = lax.axis_size("seq"), lax.axis_size("chan")
    pairs = [(s * chans + c, s * chans + (c + 1) % chans) for s in range(seqs) for c in range(chans)]
    return lax.ppermute(array, ("seq", "chan"), pairs)


def spread(own):
    units = own.shape[0]
    half = units // 2
    held = own
    pieces = []
    for step in range(1, lax.axis_size("chan")):
        held = shift(held)
        near = swap(held, NEAR)
        far = swap(held, FAR)
        low = swap(far[:half], NEAR)
        high = swap(near[half:], FAR)
        for chip, first, array in ((0, 0, held), (1, 0, near), (2, 0, far), (3, 0, low), (3, half, high)):
            pieces.append(((step, chip, 0, first, array.shape[0]), array))
            pieces.append(((step, chip, 1, first, array.shape[0]), swap(array, CORE)))
    return tuple(p[0] for p in pieces), tuple(p[1] for p in pieces)


def own_slice(units, per_chip):
    core, chip = place()
    rows = units.shape[1] // 2
    return lax.dynamic_slice(units, (chip * per_chip, core * rows, 0), (per_chip, rows, units.shape[2]))


def load_weights(meta, per_chip, chans, own, pieces, weights, sems):
    core, chip = place()
    chan = lax.axis_index("chan")
    copies = []
    for ref, first, start, count in own:
        depth = ref.shape[1]
        base = pl.multiple_of(chan * depth, 16)
        copies.append((ref.at[pl.ds(first, count)], weights.at[pl.ds(start, count), pl.ds(base, depth), :]))
    for (step, chip_mask, core_mask, first, count), ref in zip(meta, pieces):
        depth = ref.shape[1]
        shard = lax.rem(chan + chans - step, chans)
        start = (chip ^ chip_mask) * per_chip + first
        base = pl.multiple_of(shard * (2 * depth) + (core ^ core_mask) * depth, 16)
        copies.append((ref, weights.at[pl.ds(start, count), pl.ds(base, depth), :]))
    started = [pltpu.make_async_copy(src, dst, sems.at[i]) for i, (src, dst) in enumerate(copies)]
    for copy in started:
        copy.start()

    def wait():
        for copy in started:
            copy.wait()

    return wait


def inside(rows, width, first_row, first_col, height):
    row = first_row + lax.broadcasted_iota(jnp.int32, (rows, width, 1), 0)
    col = first_col + lax.broadcasted_iota(jnp.int32, (rows, width, 1), 1)
    ok = (row >= 0) & (row < height) & (col >= 0) & (col < LAT_W)
    return jnp.where(ok, 1.0, 0.0).astype(jnp.float32).reshape(rows * width, 1)


def norm_act(values, gain, shift_by, mask):
    mean_sq = jnp.mean(values * values, axis=1, keepdims=True)
    scaled = values * lax.rsqrt(mean_sq + EPS) * gain + shift_by
    return scaled / (1.0 + jnp.exp(-scaled)) * mask


def set_columns(cols, values):
    cells, chans = values.shape
    cols[:cells, :chans] = pltpu.roll(values, 1, 0).astype(jnp.bfloat16)
    cols[:cells, chans : 2 * chans] = values.astype(jnp.bfloat16)
    cols[:cells, 2 * chans :] = pltpu.roll(values, cells - 1, 0).astype(jnp.bfloat16)


def conv(cols, weights, unit, rows, width):
    chans = weights.shape[1]
    total = None
    for row_tap in range(3):
        taps = weights[unit + 3 * row_tap : unit + 3 * row_tap + 3].reshape(3 * chans, chans)
        part = jnp.dot(
            cols[row_tap * width : (row_tap + rows) * width, :], taps, preferred_element_type=jnp.float32
        )
        total = part if total is None else total + part
    return total


def res_block(stream, rows, width, block, unit, params, cols, weights, corner, height, wait):
    gain, shift_by, bias = params
    first_row, first_col = corner
    mask = inside(rows, width, first_row, first_col, height)
    set_columns(cols, norm_act(stream, gain[2 * block][None], shift_by[2 * block][None], mask))
    if wait is not None:
        wait()
    middle = conv(cols, weights, unit, rows - 2, width) + bias[2 * block][None]
    mask = inside(rows - 2, width, first_row + 1, first_col, height)
    set_columns(cols, norm_act(middle, gain[2 * block + 1][None], shift_by[2 * block + 1][None], mask))
    branch = conv(cols, weights, unit + 9, rows - 4, width) + bias[2 * block + 1][None]
    kept = stream[2 * width : (rows - 2) * width]
    return (kept + branch).astype(jnp.bfloat16).astype(jnp.float32)


def tile_corner(slab_rows, tile_cols, halo):
    return (
        lax.axis_index("seq") * slab_rows - halo,
        lax.axis_index("chan") * tile_cols - HALO,
    )


def early_kernel(meta, per_chip, chans, blocks, width, slab_rows, height, n_pieces, *refs):
    stream_ref, gain, shift_by, bias, res_ref = refs[:5]
    pieces = refs[5 : 5 + n_pieces]
    out_ref, weights, cols, sems = refs[5 + n_pieces :]
    wait = load_weights(
        meta, per_chip, chans, ((res_ref, 0, 0, 18 * blocks),), pieces, weights, sems
    )
    rows = stream_ref.shape[0] // width
    halo = (rows - slab_rows) // 2
    tile_cols = LAT_W // chans
    stream = stream_ref[...].astype(jnp.float32)
    for block in range(blocks):
        stream = res_block(
            stream, rows, width, block, 18 * block, (gain, shift_by, bias), cols, weights,
            tile_corner(slab_rows, tile_cols, halo), height, wait if block == 0 else None,
        )
        rows, halo = rows - 4, halo - 2
    out_ref[...] = stream.astype(jnp.bfloat16)


def late_kernel(meta, per_chip, chans, first_block, blocks, width, slab_rows, height, n_pieces, *refs):
    stream_ref, gain, shift_by, bias, up_bias, res_ref, up_ref = refs[:7]
    pieces = refs[7 : 7 + n_pieces]
    out_ref, weights, cols, woven, sems = refs[7 + n_pieces :]
    n_units = 18 * (blocks - first_block)
    wait = load_weights(
        meta, per_chip, chans,
        ((res_ref, 18 * first_block, 0, n_units), (up_ref, 0, n_units, up_ref.shape[0])),
        pieces, weights, sems,
    )
    rows = stream_ref.shape[0] // width
    halo = (rows - slab_rows) // 2
    tile_cols = LAT_W // chans
    stream = stream_ref[...].astype(jnp.float32)
    for block in range(first_block, blocks):
        stream = res_block(
            stream, rows, width, block, 18 * (block - first_block), (gain, shift_by, bias), cols, weights,
            tile_corner(slab_rows, tile_cols, halo), height, wait if block == first_block else None,
        )
        rows, halo = rows - 4, halo - 2
    first_row, first_col = tile_corner(slab_rows, tile_cols, halo)
    framed = (stream * inside(rows, width, first_row, first_col, height)).astype(jnp.bfloat16)
    outs = up_bias.shape[1]
    products = []
    for pair in range(5):
        both = jnp.dot(framed, weights[n_units + pair], preferred_element_type=jnp.float32)
        products += [both[:, :outs], both[:, outs:]]
    cells = rows * width
    even, odd = [], []
    for row_tap in range(3):
        left, mid, right = products[3 * row_tap : 3 * row_tap + 3]
        even.append(pltpu.roll(left, 1, 0) + mid + right)
        odd.append(left + mid + pltpu.roll(right, cells - 1, 0))
    share = outs // chans
    for row in range(slab_rows):
        for low in range(2):
            for parity, parts in ((0, even), (1, odd)):
                total = up_bias[...]
                for row_tap in range(3):
                    at = (row + 1 + (low + row_tap - 1) // 2) * width + HALO
                    total = total + parts[row_tap][at : at + tile_cols]
                for tile in range(woven.shape[0]):
                    lanes = total[:, 128 * tile : 128 * tile + 128]
                    if lanes.shape[1] < 128:
                        blank = jnp.zeros((tile_cols, 128 - lanes.shape[1]), jnp.float32)
                        lanes = jnp.concatenate([lanes, blank], 1)
                    woven[tile, pl.ds(parity, tile_cols, 2), :] = lanes
            turned = jnp.concatenate([woven[tile].T for tile in range(woven.shape[0])], 0)
            for owner in range(chans):
                out_ref[owner, 2 * row + low] = turned[owner * share : (owner + 1) * share].astype(jnp.bfloat16)


def call(kernel, args, n_vmem, out_shape, scratch, flops):
    vmem = pl.BlockSpec(memory_space=pltpu.VMEM)
    return pl.pallas_call(
        kernel,
        out_shape=out_shape,
        in_specs=[vmem] * n_vmem + [pl.BlockSpec(memory_space=pl.ANY)] * (len(args) - n_vmem),
        out_specs=vmem,
        scratch_shapes=scratch,
        compiler_params=pltpu.CompilerParams(vmem_limit_bytes=VMEM_BYTES),
        cost_estimate=pl.CostEstimate(flops=flops, bytes_accessed=16 * 1024 * 1024, transcendentals=0),
    )(*args)


def body(
    latent, in_weight, in_bias, norm_gain, norm_shift, res_weight, res_bias, up_weight, up_bias
):
    seqs, chans = lax.axis_size("seq"), lax.axis_size("chan")
    seq, chan = lax.axis_index("seq"), lax.axis_index("chan")
    layers, _, taps, depth, ch = res_weight.shape
    outs = up_weight.shape[2]
    tokens, lat_share = latent.shape[0], latent.shape[1] // chans
    slab_rows = tokens * chans // LAT_W
    height = slab_rows * seqs
    tile_cols = LAT_W // chans
    width = -(-(tile_cols + 2 * HALO) // 16) * 16
    early = layers - 1

    res_units = res_weight.reshape(layers * 2 * taps, depth, ch)
    per_early = early * 2 * taps // 4
    early_meta, early_pieces = spread(own_slice(res_units[: early * 2 * taps], per_early))
    up_units = jnp.pad(up_weight, ((0, 1), (0, 0), (0, 0))).reshape(-1, 2, depth, outs)
    up_units = up_units.transpose(0, 2, 1, 3).reshape(-1, depth, 2 * outs)
    late_units = jnp.concatenate([res_units[early * 2 * taps :], up_units], 0)
    per_late = -(-late_units.shape[0] // 4)
    late_units = jnp.pad(late_units, ((0, 4 * per_late - late_units.shape[0]), (0, 0), (0, 0)))
    late_meta, late_pieces = spread(own_slice(late_units, per_late))

    smalls = [in_weight, in_bias, norm_gain, norm_shift, res_bias, up_bias, latent]
    flat = jnp.concatenate([a.astype(jnp.float32).reshape(-1) for a in smalls])
    flat = jnp.pad(flat, (0, -flat.shape[0] % 1024))
    packed = lax.all_gather(flat, "chan")
    found, at = [], 0
    for a in smalls:
        found.append(packed[:, at : at + a.size].reshape((chans,) + a.shape))
        at += a.size
    in_w = found[0].transpose(1, 0, 2, 3).reshape(taps * lat_share * chans, ch).astype(jnp.bfloat16)
    in_b = found[1].reshape(ch)
    gain, shift_by, bias = (f.transpose(1, 2, 0, 3).reshape(2 * layers, ch) for f in found[2:5])
    up_b = found[5].reshape(1, outs)
    slab = found[6].astype(jnp.bfloat16).reshape(slab_rows * LAT_W, lat_share * chans)
    frame = lax.all_gather(slab, "seq", tiled=True).reshape(height, LAT_W, lat_share * chans)
    rows = slab_rows + 2 * (HALO - 1)
    framed = jnp.pad(frame, ((HALO, HALO), (HALO + 1, width - tile_cols - HALO + 1), (0, 0)))
    region = lax.dynamic_slice(
        framed, (seq * slab_rows, chan * tile_cols, 0), (rows + 2, width + 2, framed.shape[2])
    )
    patches = jnp.concatenate(
        [region[p : p + rows, r : r + width] for p in range(3) for r in range(3)], axis=2
    ).reshape(rows * width, -1)
    stream = (jnp.dot(patches, in_w, preferred_element_type=jnp.float32) + in_b).astype(jnp.bfloat16)

    def flops(first, blocks):
        cells = sum(slab_rows + 2 * (2 * layers - i) for i in range(2 * first + 1, 2 * blocks + 1)) * width
        return 2 * taps * ch * ch * cells

    early_args = [stream, gain, shift_by, bias, res_units, *early_pieces]
    mid_rows = rows - 4 * early
    stream = call(
        functools.partial(
            early_kernel, early_meta, per_early, chans, early, width, slab_rows, height, len(early_pieces)
        ),
        early_args, 4, jax.ShapeDtypeStruct((mid_rows * width, ch), jnp.bfloat16),
        [
            pltpu.VMEM((4 * per_early, ch, ch), jnp.bfloat16),
            pltpu.VMEM((rows * width, 3 * ch), jnp.bfloat16),
            pltpu.SemaphoreType.DMA((1 + len(early_pieces),)),
        ],
        flops(0, early),
    )
    late_args = [stream, gain, shift_by, bias, up_b, res_units, up_units, *late_pieces]
    shares = call(
        functools.partial(
            late_kernel, late_meta, per_late, chans, early, layers, width, slab_rows, height, len(late_pieces)
        ),
        late_args, 5, jax.ShapeDtypeStruct((chans, 2 * slab_rows, outs // chans, 2 * tile_cols), jnp.bfloat16),
        [
            pltpu.VMEM((4 * per_late, ch, ch), jnp.bfloat16),
            pltpu.VMEM((mid_rows * width, 3 * ch), jnp.bfloat16),
            pltpu.VMEM((-(-outs // 128), 2 * tile_cols, 128), jnp.float32),
            pltpu.SemaphoreType.DMA((2 + len(late_pieces),)),
        ],
        flops(early, layers),
    )
    turned = lax.all_to_all(shares, "chan", 0, 0, tiled=True)
    return turned.transpose(2, 1, 0, 3).reshape(outs // chans, 2 * slab_rows, 2 * LAT_W)


def solution(mesh):
    placed = (
        P(("seq", "chan"), None),
        P(None, "chan", None),
        P("chan"),
        P(None, None, "chan"),
        P(None, None, "chan"),
        P(None, None, None, "chan", None),
        P(None, None, "chan"),
        P(None, "chan", None),
        P("chan"),
    )
    return jax.shard_map(
        body, mesh=mesh, in_specs=placed, out_specs=P("chan", "seq", None), check_vma=False
    )
```

```python
import functools
import jax
import jax.numpy as jnp
from jax import lax
from jax.experimental import pallas as pl
from jax.experimental.pallas import tpu as pltpu
from jax.sharding import PartitionSpec as P

LAT_W = 256
EPS = 1e-06
HALO = 8
VMEM_BYTES = 60 * 1024 * 1024

CORE, NEAR, FAR = 1, 2, 4


def place():
    seq = lax.axis_index("seq")
    return lax.rem(seq, 2), lax.rem(lax.div(seq, 2), 4)


def swap(array, mask, chan_mask=0):
    seqs, chans = lax.axis_size("seq"), lax.axis_size("chan")
    pairs = [(s * chans + c, (s ^ mask) * chans + (c ^ chan_mask)) for s in range(seqs) for c in range(chans)]
    return lax.ppermute(array, ("seq", "chan"), pairs)


def shift(array):
    seqs, chans = lax.axis_size("seq"), lax.axis_size("chan")
    pairs = [(s * chans + c, s * chans + (c + 1) % chans) for s in range(seqs) for c in range(chans)]
    return lax.ppermute(array, ("seq", "chan"), pairs)


def in_order(found):
    chans, chan = lax.axis_size("chan"), lax.axis_index("chan")
    found = jnp.stack(found)
    return jnp.stack(
        [lax.dynamic_index_in_dim(found, lax.rem(chan + chans - c, chans), 0, False) for c in range(chans)]
    )


def gather_frame(held):
    mask = 1
    while mask < lax.axis_size("seq"):
        held = jnp.concatenate([held, swap(held, mask)], 0)
        mask *= 2
    return held


def thirds(values):
    parts = []
    for _ in range(3):
        part = lax.reduce_precision(values, 8, 7)
        parts.append(part.astype(jnp.bfloat16))
        values = values - part
    return parts


def spread(own, small, finish):
    held, small_held, found, metas, pieces = own, small, [small], [], []
    cut, steps = own.shape[0] // 2, lax.axis_size("chan") - 1
    for step in range(1, steps + 1):
        held, small_held = lax.optimization_barrier((shift(held), small_held))
        small_held = shift(small_held)
        found.append(small_held)
        near = swap(held, NEAR)
        far = swap(held, FAR)
        if step < steps:
            cross = [(0, swap(far[:cut], NEAR)), (cut, swap(near[cut:], FAR))]
        else:
            cross = [(0, swap(held, NEAR | FAR))]
            near, beside = lax.optimization_barrier((near, finish(in_order(found))))
        arrays = [(0, 0, held), (NEAR // 2, 0, near), (FAR // 2, 0, far)]
        arrays += [((NEAR | FAR) // 2, first, array) for first, array in cross]
        for chip, first, array in arrays:
            for core in range(2):
                metas.append((chip, core, step, first))
                pieces.append(swap(array, CORE) if core else array)
    return tuple(metas), pieces, beside


def own_slice(units, per_chip):
    core, chip = place()
    rows = units.shape[1] // 2
    return lax.dynamic_slice(units, (chip * per_chip, core * rows, 0), (per_chip, rows, units.shape[2]))


def load_weights(metas, per_chip, chans, own, pieces, weights, sems):
    core, chip = place()
    chan = lax.axis_index("chan")
    depth = own[0][0].shape[1]
    half = depth // 2
    for ref, begin in own:
        at = 0
        while at < ref.shape[0]:
            owner = (begin + at) // per_chip
            count = min(ref.shape[0] - at, (owner + 1) * per_chip - begin - at)
            base = pl.multiple_of(chan * depth, 16)
            dst = weights.at[pl.ds(begin + at, count), pl.ds(base, depth), :]
            pltpu.make_async_copy(ref.at[pl.ds(at, count)], dst, sems.at[owner, 0]).start()
            at += count
    total = sum(ref.shape[0] for ref, _ in own)
    for (chip_mask, core_mask, step, first), ref in zip(metas, pieces):
        shard = lax.rem(chan + chans - step, chans)
        owner = chip ^ chip_mask
        base = pl.multiple_of(shard * depth + (core ^ core_mask) * half, 16)
        dst = weights.at[pl.ds(owner * per_chip + first, ref.shape[0]), pl.ds(base, half), :]
        pltpu.make_async_copy(ref, dst, sems.at[owner, 2 * step - 1 + core_mask]).start()

    def wait(owner):
        begin = owner * per_chip
        mine = weights.at[pl.ds(begin, min(per_chip, total - begin)), pl.ds(0, depth), :]
        pltpu.make_async_copy(mine, mine, sems.at[owner, 0]).wait()
        slice_of = weights.at[pl.ds(begin, per_chip), pl.ds(0, half), :]
        for i in range(1, 2 * chans - 1):
            pltpu.make_async_copy(slice_of, slice_of, sems.at[owner, i]).wait()

    return wait


def inside(rows, width, first_row, first_col, height):
    row = first_row + lax.broadcasted_iota(jnp.int32, (rows, width, 1), 0)
    col = first_col + lax.broadcasted_iota(jnp.int32, (rows, width, 1), 1)
    ok = (row >= 0) & (row < height) & (col >= 0) & (col < LAT_W)
    return jnp.where(ok, 1.0, 0.0).astype(jnp.float32).reshape(rows * width, 1)


def norm_act(values, gain, shift_by, mask):
    mean_sq = jnp.mean(values * values, axis=1, keepdims=True)
    scaled = values * lax.rsqrt(mean_sq + EPS) * gain + shift_by
    return scaled / (1.0 + jnp.exp(-scaled)) * mask


def set_columns(cols, values):
    cells, chans = values.shape
    cols[:cells, :chans] = pltpu.roll(values, 1, 0).astype(jnp.bfloat16)
    cols[:cells, chans : 2 * chans] = values.astype(jnp.bfloat16)
    cols[:cells, 2 * chans :] = pltpu.roll(values, cells - 1, 0).astype(jnp.bfloat16)


def conv(cols, weights, unit, rows, width):
    chans = weights.shape[1]
    total = None
    for row_tap in range(3):
        taps = weights[unit + 3 * row_tap : unit + 3 * row_tap + 3].reshape(3 * chans, chans)
        part = jnp.dot(
            cols[row_tap * width : (row_tap + rows) * width, :], taps, preferred_element_type=jnp.float32
        )
        total = part if total is None else total + part
    return total


def res_block(stream, rows, width, block, params, cols, weights, corner, height, need):
    gain, shift_by, bias = params
    first_row, first_col = corner
    mask = inside(rows, width, first_row, first_col, height)
    set_columns(cols, norm_act(stream, gain[2 * block][None], shift_by[2 * block][None], mask))
    unit = 18 * block
    need(unit + 9)
    middle = conv(cols, weights, unit, rows - 2, width) + bias[2 * block][None]
    mask = inside(rows - 2, width, first_row + 1, first_col, height)
    set_columns(cols, norm_act(middle, gain[2 * block + 1][None], shift_by[2 * block + 1][None], mask))
    need(unit + 18)
    branch = conv(cols, weights, unit + 9, rows - 4, width) + bias[2 * block + 1][None]
    kept = stream[2 * width : (rows - 2) * width]
    return (kept + branch).astype(jnp.bfloat16).astype(jnp.float32)


def tile_corner(slab_rows, tile_cols, halo):
    return (
        lax.axis_index("seq") * slab_rows - halo,
        lax.axis_index("chan") * tile_cols - HALO,
    )


def enter(frame, in_weight, in_bias, rows, width, slab_rows, height, tile_cols, slab, wide, in_cols, sems):
    lat, tokens = frame.shape[1:]
    blocks = LAT_W // tokens
    first_row, first_col = tile_corner(slab_rows, tile_cols, HALO)
    fetches = []
    for row in range(rows + 2):
        held = (first_row + row >= 0) & (first_row + row < height)
        at = jnp.clip(first_row + row, 0, height - 1)
        owner = lax.div(at, slab_rows) ^ lax.axis_index("seq")
        start = (owner * slab_rows + lax.rem(at, slab_rows)) * blocks
        fetch = pltpu.make_async_copy(frame.at[pl.ds(start, blocks)], slab.at[row], sems.at[row])
        fetches.append((held, fetch))

    def start_all():
        for held, fetch in fetches:
            pl.when(held)(fetch.start)

    def finish():
        for held, fetch in fetches:
            pl.when(held)(fetch.wait)
        for row in range(rows + 2):
            for block in range(blocks):
                wide[row, 2 * HALO + block * tokens : 2 * HALO + (block + 1) * tokens, :] = slab[row, block].astype(jnp.float32).T
        left = pl.multiple_of(lax.axis_index("chan") * tile_cols + HALO, 8)
        region = wide[:, pl.ds(left, width), :].reshape((rows + 2) * width, lat)
        mask = inside(rows + 2, width, first_row, first_col, height)
        set_columns(in_cols, jnp.where(mask > 0.0, region, 0.0))
        total = in_bias[...]
        for row_tap in range(3):
            part = in_cols[row_tap * width : (row_tap + rows) * width, :]
            total = total + jnp.dot(part, in_weight[row_tap], preferred_element_type=jnp.float32)
        return total.astype(jnp.bfloat16).astype(jnp.float32)

    return start_all, finish


def tile_kernel(static, *refs):
    chans, layers, rows, width, slab_rows, height, metas, per_chip = static
    gain, shift_by, bias, in_w, in_b, up_bias, frame, res_ref, up_ref = refs[:9]
    pieces = refs[9 : 9 + len(metas)]
    out_ref, weights, cols, slab, wide, in_cols, woven, slab_sems, sems = refs[9 + len(metas) :]
    tile_cols = LAT_W // chans
    start_all, finish = enter(
        frame, in_w, in_b, rows, width, slab_rows, height, tile_cols, slab, wide, in_cols, slab_sems
    )
    start_all()
    n_res = res_ref.shape[0]
    wait = load_weights(metas, per_chip, chans, ((res_ref, 0), (up_ref, n_res)), pieces, weights, sems)
    waited = [0]

    def need(units):
        while waited[0] * per_chip < units:
            wait(waited[0])
            waited[0] += 1

    halo = (rows - slab_rows) // 2
    stream = finish()
    for layer in range(layers):
        stream = res_block(
            stream, rows, width, layer, (gain, shift_by, bias), cols, weights,
            tile_corner(slab_rows, tile_cols, halo), height, need,
        )
        rows, halo = rows - 4, halo - 2
    need(n_res + up_ref.shape[0])
    first_row, first_col = tile_corner(slab_rows, tile_cols, halo)
    framed = (stream * inside(rows, width, first_row, first_col, height)).astype(jnp.bfloat16)
    outs = up_bias.shape[1]
    products = []
    for pair in range(up_ref.shape[0]):
        both = jnp.dot(framed, weights[n_res + pair], preferred_element_type=jnp.float32)
        products += [both[:, :outs], both[:, outs:]]
    cells = rows * width
    even, odd = [], []
    for row_tap in range(3):
        left, mid, right = products[3 * row_tap : 3 * row_tap + 3]
        even.append(pltpu.roll(left, 1, 0) + mid + right)
        odd.append(left + mid + pltpu.roll(right, cells - 1, 0))
    share = outs // chans
    for row in range(slab_rows):
        for low in range(2):
            for parity, parts in ((0, even), (1, odd)):
                total = up_bias[...]
                for row_tap in range(3):
                    at = (row + 1 + (low + row_tap - 1) // 2) * width + HALO
                    total = total + parts[row_tap][at : at + tile_cols]
                for tile in range(woven.shape[0]):
                    lanes = total[:, 128 * tile : 128 * tile + 128]
                    if lanes.shape[1] < 128:
                        blank = jnp.zeros((tile_cols, 128 - lanes.shape[1]), jnp.float32)
                        lanes = jnp.concatenate([lanes, blank], 1)
                    woven[tile, pl.ds(parity, tile_cols, 2), :] = lanes
            turned = jnp.concatenate([woven[tile].T for tile in range(woven.shape[0])], 0)
            for owner in range(chans):
                out_ref[owner, 2 * row + low] = turned[owner * share : (owner + 1) * share].astype(jnp.bfloat16)


def body(
    latent, in_weight, in_bias, norm_gain, norm_shift, res_weight, res_bias, up_weight, up_bias
):
    seqs, chans = lax.axis_size("seq"), lax.axis_size("chan")
    layers, _, taps, depth, ch = res_weight.shape
    outs = up_weight.shape[2]
    tokens, lat = latent.shape
    slab_rows = tokens * chans // LAT_W
    height = slab_rows * seqs
    tile_cols = LAT_W // chans
    width = -(-(tile_cols + 2 * HALO) // 16) * 16

    norms = [a.reshape(2 * layers, depth) for a in (norm_gain, norm_shift, res_bias)]
    ends = jnp.zeros((2 * layers, depth), jnp.float32)
    ends = ends.at[0].set(in_bias).at[1, : outs // chans].set(up_bias)
    smalls = [*thirds(jnp.concatenate(norms + [ends], 1)), in_weight.reshape(-1, ch)]
    smalls = jnp.concatenate(smalls, 0)
    n_small = smalls.shape[0]
    smalls = [smalls[:, at : at + tokens] for at in range(0, ch, tokens)]
    smalls = jnp.concatenate([*smalls, gather_frame(latent.T[None]).reshape(-1, tokens)], 0)

    def small_args(packed):
        n_lanes = ch // tokens
        frame = packed[:, n_small * n_lanes :].reshape(chans, seqs, lat, tokens).transpose(1, 0, 2, 3)
        frame = frame.reshape(seqs * chans, lat, tokens)
        packed = jnp.concatenate([packed[:, n_small * i : n_small * (i + 1)] for i in range(n_lanes)], 2)
        params = sum(packed[:, 2 * layers * i : 2 * layers * (i + 1)].astype(jnp.float32) for i in range(3))
        params = params.reshape(chans, 2 * layers, 4, depth).transpose(2, 1, 0, 3)
        gain, shift_by, bias = (params[i].reshape(2 * layers, ch) for i in range(3))
        in_b = params[3, 0].reshape(1, ch)
        up_b = params[3, 1, :, : outs // chans].reshape(1, outs)
        in_w = packed[:, 6 * layers :].reshape(chans, 3, taps // 3, lat // chans, ch)
        in_w = in_w.transpose(1, 2, 0, 3, 4).reshape(3, taps // 3 * lat, ch)
        return gain, shift_by, bias, in_w, in_b, up_b, frame

    res_units = res_weight.reshape(layers * 2 * taps, depth, ch)
    up_units = jnp.pad(up_weight, ((0, 1), (0, 0), (0, 0))).reshape(-1, 2, depth, outs)
    up_units = up_units.transpose(0, 2, 1, 3).reshape(-1, depth, 2 * outs)
    units = jnp.concatenate([res_units, up_units], 0)
    per_chip = -(-units.shape[0] // 4)
    units = jnp.pad(units, ((0, 4 * per_chip - units.shape[0]), (0, 0), (0, 0)))
    metas, pieces, small = spread(own_slice(units, per_chip), smalls, small_args)

    rows = slab_rows + 2 * (HALO - 1)
    in_vmem = small[:-1]
    in_any = [small[-1], res_units, up_units, *pieces]
    vmem = pl.BlockSpec(memory_space=pltpu.VMEM)
    cells = sum(rows - 2 * i for i in range(1, 2 * layers + 1)) * width
    shares = pl.pallas_call(
        functools.partial(
            tile_kernel, (chans, layers, rows, width, slab_rows, height, metas, per_chip)
        ),
        out_shape=jax.ShapeDtypeStruct((chans, 2 * slab_rows, outs // chans, 2 * tile_cols), jnp.bfloat16),
        in_specs=[vmem] * len(in_vmem) + [pl.BlockSpec(memory_space=pl.ANY)] * len(in_any),
        out_specs=vmem,
        scratch_shapes=[
            pltpu.VMEM((4 * per_chip, ch, ch), jnp.bfloat16),
            pltpu.VMEM((rows * width, 3 * ch), jnp.bfloat16),
            pltpu.VMEM((rows + 2, LAT_W // tokens, lat, tokens), jnp.bfloat16),
            pltpu.VMEM((rows + 2, LAT_W + 4 * HALO, lat), jnp.float32),
            pltpu.VMEM(((rows + 2) * width, 3 * lat), jnp.bfloat16),
            pltpu.VMEM((-(-outs // 128), 2 * tile_cols, 128), jnp.float32),
            pltpu.SemaphoreType.DMA((rows + 2,)),
            pltpu.SemaphoreType.DMA((4, 2 * chans - 1)),
        ],
        compiler_params=pltpu.CompilerParams(vmem_limit_bytes=VMEM_BYTES),
        cost_estimate=pl.CostEstimate(
            flops=2 * taps * ch * ch * cells, bytes_accessed=4 * per_chip * ch * ch * 2, transcendentals=0
        ),
    )(*in_vmem, *in_any)
    turned = lax.all_to_all(shares, "chan", 0, 0, tiled=True)
    return turned.transpose(2, 1, 0, 3).reshape(outs // chans, 2 * slab_rows, 2 * LAT_W)


def solution(mesh):
    placed = (
        P(("seq", "chan"), None),
        P(None, "chan", None),
        P("chan"),
        P(None, None, "chan"),
        P(None, None, "chan"),
        P(None, None, None, "chan", None),
        P(None, None, "chan"),
        P(None, "chan", None),
        P("chan"),
    )
    return jax.shard_map(
        body, mesh=mesh, in_specs=placed, out_specs=P("chan", "seq", None), check_vma=False
    )
```

```python
import functools
import jax
import jax.numpy as jnp
from jax import lax
from jax.experimental import pallas as pl
from jax.experimental.pallas import tpu as pltpu
from jax.sharding import PartitionSpec as P

LAT_W = 256
EPS = 1e-06
HALO = 8
CHUNK = 3
VMEM_BYTES = 60 * 1024 * 1024
ENTER_VMEM = 16 * 1024 * 1024

CORE, NEAR, FAR = 1, 2, 4


def place():
    seq = lax.axis_index("seq")
    return lax.rem(seq, 2), lax.rem(lax.div(seq, 2), 4)


def swap(array, mask, chan_mask=0):
    seqs, chans = lax.axis_size("seq"), lax.axis_size("chan")
    pairs = [(s * chans + c, (s ^ mask) * chans + (c ^ chan_mask)) for s in range(seqs) for c in range(chans)]
    return lax.ppermute(array, ("seq", "chan"), pairs)


def shift(array, steps=1):
    seqs, chans = lax.axis_size("seq"), lax.axis_size("chan")
    pairs = [(s * chans + c, s * chans + (c + steps) % chans) for s in range(seqs) for c in range(chans)]
    return lax.ppermute(array, ("seq", "chan"), pairs)


def in_order(found):
    chans, chan = lax.axis_size("chan"), lax.axis_index("chan")
    found = jnp.stack(found)
    return jnp.stack(
        [lax.dynamic_index_in_dim(found, lax.rem(chan + chans - c, chans), 0, False) for c in range(chans)]
    )


def gather_frame(held):
    mask = 1
    while mask < lax.axis_size("seq"):
        held = jnp.concatenate([held, swap(held, mask)], 0)
        mask *= 2
    return held


def thirds(values):
    parts = []
    for _ in range(3):
        part = lax.reduce_precision(values, 8, 7)
        parts.append(part.astype(jnp.bfloat16))
        values = values - part
    return parts


def spread(own, small, finish, early):
    units = own.shape[0]
    cut, third = units // 2, (units - early) // 3
    mid, end = early + third, early + 2 * third
    x, y, across = NEAR // 2, FAR // 2, (NEAR | FAR) // 2
    settle = lax.optimization_barrier
    pieces = []

    def add(array, *parts):
        twin = swap(array, CORE)
        pieces.extend([(0, parts, array), (1, parts, twin)])
        return twin

    held_1, small_1 = settle((shift(own), shift(small)))
    held_2, small_2 = shift(held_1), shift(small_1)
    near_1, far_1 = swap(held_1, NEAR), swap(held_1, FAR)
    twin = add(held_1, (0, 1, 0, units))
    held_2, small_2, near_1, far_1, twin = settle((held_2, small_2, near_1, far_1, twin))
    held_3, small_3 = shift(held_2), shift(small_2)
    near_2 = swap(jnp.concatenate([held_2, far_1[:cut]], 0), NEAR)
    far_2 = swap(jnp.concatenate([held_2, near_1[cut:]], 0), FAR)
    twins = [
        add(near_1, (x, 1, 0, units)), add(far_1, (y, 1, 0, units)), add(held_2, (0, 2, 0, units)),
    ]
    held_3, small_3, near_2, far_2, twins = settle((held_3, small_3, near_2, far_2, twins))
    across_2 = shift(jnp.concatenate([near_2[units:], far_2[units:]], 0))
    near_3, far_3, first_3 = swap(held_3, NEAR), swap(held_3, FAR), swap(held_3[:early], NEAR | FAR)
    twins = [
        add(near_2, (x, 2, 0, units), (across, 1, 0, cut)),
        add(far_2, (y, 2, 0, units), (across, 1, cut, units - cut)),
        add(held_3, (0, 3, 0, units)),
    ]
    across_2, near_3, far_3, first_3, twins, extra = settle(
        (across_2, near_3, far_3, first_3, twins, finish(in_order([small, small_1, small_2, small_3])))
    )
    add(near_3, (x, 3, 0, units))
    add(far_3, (y, 3, 0, units))
    add(across_2, (across, 2, 0, units))
    add(first_3, (across, 3, 0, early))
    late = [
        (swap(far_3[early:mid], NEAR), (across, 3, early, third)),
        (swap(near_3[mid:end], FAR), (across, 3, mid, third)),
        (shift(across_2[end:]), (across, 3, end, units - end)),
    ]

    def last(gate):
        for array, part in late:
            add(settle((array, gate))[0], part)
        return pieces

    return pieces, last, extra


def groups_of(low, high, per_early, per_late):
    found = []
    for begin, per_chip, at in ((0, per_early, 0), (4 * per_early, per_late, per_early)):
        for chip in range(4):
            first = begin + chip * per_chip
            lowest, highest = max(first, low), min(first + per_chip, high)
            if lowest < highest:
                found.append((chip, at + lowest - first, lowest, highest - lowest))
    return tuple(found)


def own_slice(units, per_chip):
    core, chip = place()
    rows = units.shape[1] // 2
    return lax.dynamic_slice(units, (chip * per_chip, core * rows, 0), (per_chip, rows, units.shape[2]))


def load_weights(groups, metas, chans, own, pieces, weights, sems):
    core, chip = place()
    chan = lax.axis_index("chan")
    base = groups[0][2]
    depth = own[0][0].shape[1]
    half = depth // 2

    def start_own(group, unit, units):
        at = pl.multiple_of(chan * depth, 16)
        for ref, begin in own:
            first, end = max(unit, begin), min(unit + units, begin + ref.shape[0])
            if first < end:
                dst = weights.at[pl.ds(first - base, end - first), pl.ds(at, depth), :]
                src = ref.at[pl.ds(first - begin, end - first)]
                pltpu.make_async_copy(src, dst, sems.at[group, 0]).start()

    def start_others(group, place_in, unit, units, chip_mask):
        for (core_mask, parts), ref in zip(metas, pieces):
            at = 0
            for mask, step, first, count in parts:
                low, high = max(first, place_in), min(first + count, place_in + units)
                if mask == chip_mask and low < high:
                    shard = lax.rem(chan + chans - step, chans)
                    row = pl.multiple_of(shard * depth + (core ^ core_mask) * half, 16)
                    to = unit - base + low - place_in
                    dst = weights.at[pl.ds(to, high - low), pl.ds(row, half), :]
                    src = ref.at[pl.ds(at + low - first, high - low)]
                    pltpu.make_async_copy(src, dst, sems.at[group, 2 * step - 1 + core_mask]).start()
                at += count

    for here in range(4):

        @pl.when(chip == here)
        def _():
            for group, (owner, place_in, unit, units) in enumerate(groups):
                start_own(group, unit, units)
                start_others(group, place_in, unit, units, here ^ owner)

    left = list(enumerate(groups))

    def need(end):
        while left and left[0][1][2] < end:
            group, (_, _, unit, units) = left.pop(0)
            taken = sum(
                max(0, min(unit + units, begin + ref.shape[0]) - max(unit, begin)) for ref, begin in own
            )
            mine = weights.at[pl.ds(unit - base, taken), pl.ds(0, depth), :]
            pltpu.make_async_copy(mine, mine, sems.at[group, 0]).wait()
            slice_of = weights.at[pl.ds(unit - base, units), pl.ds(0, half), :]
            for i in range(1, 2 * chans - 1):
                pltpu.make_async_copy(slice_of, slice_of, sems.at[group, i]).wait()

    return need


def inside(rows, width, first_row, first_col, height):
    row = first_row + lax.broadcasted_iota(jnp.int32, (rows, width, 1), 0)
    col = first_col + lax.broadcasted_iota(jnp.int32, (rows, width, 1), 1)
    ok = (row >= 0) & (row < height) & (col >= 0) & (col < LAT_W)
    return jnp.where(ok, 1.0, 0.0).astype(jnp.float32).reshape(rows * width, 1)


def norm_act(values, gain, shift_by, mask):
    mean_sq = jnp.mean(values * values, axis=1, keepdims=True)
    scaled = values * lax.rsqrt(mean_sq + EPS) * gain + shift_by
    half = 0.5 * scaled * mask
    return half + half * jnp.tanh(0.5 * scaled)


def set_columns(cols, values, at=0):
    cells, chans = values.shape
    cols[at : at + cells, :chans] = pltpu.roll(values, 1, 0).astype(jnp.bfloat16)
    cols[at : at + cells, chans : 2 * chans] = values.astype(jnp.bfloat16)
    cols[at : at + cells, 2 * chans :] = pltpu.roll(values, cells - 1, 0).astype(jnp.bfloat16)


def conv(cols, weights, unit, row, rows, width):
    chans = weights.shape[1]
    total = None
    for row_tap in range(3):
        taps = weights[unit + 3 * row_tap : unit + 3 * row_tap + 3].reshape(3 * chans, chans)
        at = (row + row_tap - 1) * width
        part = jnp.dot(cols[at : at + rows * width, :], taps, preferred_element_type=jnp.float32)
        total = part if total is None else total + part
    return total


def chunks(low, high):
    count = max(1, (high - low) // CHUNK)
    cuts = [low + (high - low) * i // count for i in range(count + 1)]
    return list(zip(cuts[:-1], cuts[1:]))


def tile_corner(slab_rows, tile_cols, halo):
    return (
        lax.axis_index("seq") * slab_rows - halo,
        lax.axis_index("chan") * tile_cols - HALO,
    )


def enter_kernel(static, params, in_weight, frame, out_ref, slab, wide, in_cols, sems):
    chans, rows, width, slab_rows, height = static
    tile_cols = LAT_W // chans
    lat, tokens = frame.shape[1:]
    blocks = LAT_W // tokens
    first_row, first_col = tile_corner(slab_rows, tile_cols, HALO)
    fetches = []
    for row in range(rows + 2):
        held = (first_row + row >= 0) & (first_row + row < height)
        at = jnp.clip(first_row + row, 0, height - 1)
        owner = lax.div(at, slab_rows) ^ lax.axis_index("seq")
        start = (owner * slab_rows + lax.rem(at, slab_rows)) * blocks
        fetch = pltpu.make_async_copy(frame.at[pl.ds(start, blocks)], slab.at[row], sems.at[row])
        pl.when(held)(fetch.start)
        fetches.append((held, fetch))
    for held, fetch in fetches:
        pl.when(held)(fetch.wait)
    for row in range(rows + 2):
        for block in range(blocks):
            at = 2 * HALO + block * tokens
            wide[row, at : at + tokens, :] = slab[row, block].astype(jnp.float32).T
    left = pl.multiple_of(lax.axis_index("chan") * tile_cols + HALO, 8)
    region = wide[:, pl.ds(left, width), :].reshape((rows + 2) * width, lat)
    mask = inside(rows + 2, width, first_row, first_col, height)
    set_columns(in_cols, jnp.where(mask > 0.0, region, 0.0))
    total = params[3, 0][None]
    for row_tap in range(3):
        part = in_cols[row_tap * width : (row_tap + rows) * width, :]
        total = total + jnp.dot(part, in_weight[row_tap], preferred_element_type=jnp.float32)
    out_ref[...] = total.astype(jnp.bfloat16)


def tile_kernel(static, *refs):
    chans, layers, begin, end, width, rows, slab_rows, height, groups, metas = static
    upsamples = end == layers
    params, up_bias, entered, res_ref, up_ref = refs[:5]
    pieces = refs[5 : 5 + len(metas)]
    n_outs = chans if upsamples else 1
    outs = refs[5 + len(metas) : 5 + len(metas) + n_outs]
    weights, held, cols_a, cols_b, last, woven, sems = refs[5 + len(metas) + n_outs :]
    gain, shift_by, bias = params[0], params[1], params[2]
    tile_cols = LAT_W // chans
    n_res = res_ref.shape[0]
    need = load_weights(groups, metas, chans, ((res_ref, 0), (up_ref, n_res)), pieces, weights, sems)
    base = groups[0][2]
    corner = tile_corner(slab_rows, tile_cols, (rows - slab_rows) // 2)

    def norm(values, index, row, stop):
        mask = inside(stop - row, width, corner[0] + row, corner[1], height)
        return norm_act(values, gain[index][None], shift_by[index][None], mask)

    held[...] = entered[...].astype(jnp.float32)
    for low, high in chunks(0, rows):
        set_columns(cols_a, norm(held[low * width : high * width, :], 2 * begin, low, high), low * width)
    for layer in range(begin, end):
        margin, unit = 2 * (layer - begin) + 1, 18 * layer
        need(unit + 9)
        for low, high in chunks(margin, rows - margin):
            middle = conv(cols_a, weights, unit - base, low, high - low, width) + bias[2 * layer][None]
            set_columns(cols_b, norm(middle, 2 * layer + 1, low, high), low * width)
        need(unit + 18)
        for low, high in chunks(margin + 1, rows - margin - 1):
            branch = conv(cols_b, weights, unit + 9 - base, low, high - low, width) + bias[2 * layer + 1][None]
            cells = slice(low * width, high * width)
            out_cells = slice((low - margin - 1) * width, (high - margin - 1) * width)
            stream = (held[cells, :] + branch).astype(jnp.bfloat16)
            if layer < end - 1:
                held[cells, :] = stream.astype(jnp.float32)
                set_columns(cols_a, norm(held[cells, :], 2 * layer + 2, low, high), low * width)
            elif upsamples:
                mask = inside(high - low, width, corner[0] + low, corner[1], height)
                last[out_cells, :] = (stream.astype(jnp.float32) * mask).astype(jnp.bfloat16)
            else:
                outs[0][out_cells, :] = stream
    need(n_res + up_ref.shape[0])
    if not upsamples:
        return
    framed = last[...]
    rows = framed.shape[0] // width
    n_out = up_bias.shape[1]
    products = []
    for pair in range(up_ref.shape[0]):
        both = jnp.dot(framed, weights[n_res - base + pair], preferred_element_type=jnp.float32)
        products += [both[:, :n_out], both[:, n_out:]]
    cells = rows * width
    even, odd = [], []
    for row_tap in range(3):
        left, mid, right = products[3 * row_tap : 3 * row_tap + 3]
        even.append(pltpu.roll(left, 1, 0) + mid + right)
        odd.append(left + mid + pltpu.roll(right, cells - 1, 0))
    share = n_out // chans
    chan = lax.axis_index("chan")
    for row in range(slab_rows):
        for low in range(2):
            for parity, parts in ((0, even), (1, odd)):
                total = up_bias[...]
                for row_tap in range(3):
                    at = (row + 1 + (low + row_tap - 1) // 2) * width + HALO
                    total = total + parts[row_tap][at : at + tile_cols]
                for tile in range(woven.shape[0]):
                    lanes = total[:, 128 * tile : 128 * tile + 128]
                    if lanes.shape[1] < 128:
                        blank = jnp.zeros((tile_cols, 128 - lanes.shape[1]), jnp.float32)
                        lanes = jnp.concatenate([lanes, blank], 1)
                    woven[tile, pl.ds(parity, tile_cols, 2), :] = lanes
            turned = jnp.concatenate([woven[tile].T for tile in range(woven.shape[0])], 0)
            for owner in range(chans):
                part = turned[owner * share : (owner + 1) * share].astype(jnp.bfloat16)
                for step in range(chans):

                    @pl.when(lax.rem(chan + step, chans) == owner)
                    def _():
                        outs[step][2 * row + low] = part


def body(
    latent, in_weight, in_bias, norm_gain, norm_shift, res_weight, res_bias, up_weight, up_bias
):
    seqs, chans = lax.axis_size("seq"), lax.axis_size("chan")
    layers, _, taps, depth, ch = res_weight.shape
    outs = up_weight.shape[2]
    tokens, lat = latent.shape
    slab_rows = tokens * chans // LAT_W
    height = slab_rows * seqs
    tile_cols = LAT_W // chans
    width = -(-(tile_cols + 2 * HALO) // 16) * 16
    rows = slab_rows + 2 * (HALO - 1)
    vmem = pl.BlockSpec(memory_space=pltpu.VMEM)

    norms = [a.reshape(2 * layers, depth) for a in (norm_gain, norm_shift, res_bias)]
    ends = jnp.zeros((2 * layers, depth), jnp.float32)
    ends = ends.at[0].set(in_bias).at[1, : outs // chans].set(up_bias)
    smalls = [*thirds(jnp.concatenate(norms + [ends], 1)), in_weight.reshape(-1, ch)]
    smalls = jnp.concatenate(smalls, 0)
    n_small = smalls.shape[0]
    smalls = [smalls[:, at : at + tokens] for at in range(0, ch, tokens)]
    smalls = jnp.concatenate([*smalls, gather_frame(latent.T[None]).reshape(-1, tokens)], 0)

    def small_args(packed):
        n_lanes = ch // tokens
        frame = packed[:, n_small * n_lanes :].reshape(chans, seqs, lat, tokens).transpose(1, 0, 2, 3)
        frame = frame.reshape(seqs * chans, lat, tokens)
        packed = jnp.concatenate([packed[:, n_small * i : n_small * (i + 1)] for i in range(n_lanes)], 2)
        params = sum(packed[:, 2 * layers * i : 2 * layers * (i + 1)].astype(jnp.float32) for i in range(3))
        params = params.reshape(chans, 2 * layers, 4, depth).transpose(2, 1, 0, 3)
        up_b = params[3, 1, :, : outs // chans].reshape(1, outs)
        params = params.reshape(4, 2 * layers, ch)
        in_w = packed[:, 6 * layers :].reshape(chans, 3, taps // 3, lat // chans, ch)
        in_w = in_w.transpose(1, 2, 0, 3, 4).reshape(3, taps // 3 * lat, ch)
        entered = pl.pallas_call(
            functools.partial(enter_kernel, (chans, rows, width, slab_rows, height)),
            out_shape=jax.ShapeDtypeStruct((rows * width, ch), jnp.bfloat16),
            in_specs=[vmem, vmem, pl.BlockSpec(memory_space=pl.ANY)],
            out_specs=vmem,
            scratch_shapes=[
                pltpu.VMEM((rows + 2, LAT_W // tokens, lat, tokens), jnp.bfloat16),
                pltpu.VMEM((rows + 2, LAT_W + 4 * HALO, lat), jnp.float32),
                pltpu.VMEM(((rows + 2) * width, 3 * lat), jnp.bfloat16),
                pltpu.SemaphoreType.DMA((rows + 2,)),
            ],
            compiler_params=pltpu.CompilerParams(vmem_limit_bytes=ENTER_VMEM),
        )(params, in_w, frame)
        return params, up_b, entered

    res_units = res_weight.reshape(layers * 2 * taps, depth, ch)
    up_units = jnp.pad(up_weight, ((0, 1), (0, 0), (0, 0))).reshape(-1, 2, depth, outs)
    up_units = up_units.transpose(0, 2, 1, 3).reshape(-1, depth, 2 * outs)
    n_units = res_units.shape[0] + up_units.shape[0]
    per_early = -(-2 * taps // 4)
    per_late = -(-(n_units - 4 * per_early) // 4)
    late_units = jnp.concatenate([res_units[4 * per_early :], up_units], 0)
    late_units = jnp.pad(late_units, ((0, 4 * per_late - late_units.shape[0]), (0, 0), (0, 0)))
    mine = [own_slice(res_units[: 4 * per_early], per_early), own_slice(late_units, per_late)]
    pieces, last_pieces, small = spread(jnp.concatenate(mine, 0), smalls, small_args, per_early)
    params, up_b, stream = small

    def run(begin, end, rows, stream, pieces):
        first, stop = 2 * taps * begin, 2 * taps * end
        if end == layers:
            stop = 4 * (per_early + per_late)
            out_shape, n_out = (2 * slab_rows, outs // chans, 2 * tile_cols), chans
        else:
            out_shape, n_out = ((rows - 4 * (end - begin)) * width, ch), 1
        groups = groups_of(first, stop, per_early, per_late)
        metas = tuple((core, parts) for core, parts, _ in pieces)
        in_vmem = [params, up_b, stream]
        in_any = [res_units, up_units] + [array for _, _, array in pieces]
        cells = sum(rows - 2 * i for i in range(1, 2 * (end - begin) + 1)) * width
        return pl.pallas_call(
            functools.partial(
                tile_kernel, (chans, layers, begin, end, width, rows, slab_rows, height, groups, metas)
            ),
            out_shape=[jax.ShapeDtypeStruct(out_shape, jnp.bfloat16)] * n_out,
            in_specs=[vmem] * len(in_vmem) + [pl.BlockSpec(memory_space=pl.ANY)] * len(in_any),
            out_specs=[vmem] * n_out,
            scratch_shapes=[
                pltpu.VMEM((stop - first, ch, ch), jnp.bfloat16),
                pltpu.VMEM((rows * width, ch), jnp.float32),
                pltpu.VMEM((rows * width, 3 * ch), jnp.bfloat16),
                pltpu.VMEM((rows * width, 3 * ch), jnp.bfloat16),
                pltpu.VMEM(((slab_rows + 2) * width, ch), jnp.bfloat16),
                pltpu.VMEM((-(-outs // 128), 2 * tile_cols, 128), jnp.float32),
                pltpu.SemaphoreType.DMA((len(groups), 2 * chans - 1)),
            ],
            compiler_params=pltpu.CompilerParams(vmem_limit_bytes=VMEM_BYTES),
            cost_estimate=pl.CostEstimate(
                flops=4 * taps * ch * ch * cells, bytes_accessed=(stop - first) * ch * ch * 2, transcendentals=0
            ),
        )(*in_vmem, *in_any)

    [stream] = run(0, 1, rows, stream, pieces)
    shares = run(1, layers, rows - 4, stream, last_pieces(stream))
    shares = in_order([shares[0]] + [shift(shares[step], step) for step in range(1, chans)])
    return shares.transpose(2, 1, 0, 3).reshape(outs // chans, 2 * slab_rows, 2 * LAT_W)


def solution(mesh):
    placed = (
        P(("seq", "chan"), None),
        P(None, "chan", None),
        P("chan"),
        P(None, None, "chan"),
        P(None, None, "chan"),
        P(None, None, None, "chan", None),
        P(None, None, "chan"),
        P(None, "chan", None),
        P("chan"),
    )
    return jax.shard_map(
        body, mesh=mesh, in_specs=placed, out_specs=P("chan", "seq", None), check_vma=False
    )
```

```python
import functools
import jax
import jax.numpy as jnp
from jax import lax
from jax.experimental import pallas as pl
from jax.experimental.pallas import tpu as pltpu
from jax.sharding import PartitionSpec as P

LAT_W = 256
EPS = 1e-06
HALO = 8
CHUNK = 2
AHEAD = 2
VMEM_BYTES = 60 * 1024 * 1024
ENTER_VMEM = 16 * 1024 * 1024

CORE, NEAR, FAR = 1, 2, 4


def place():
    seq = lax.axis_index("seq")
    return lax.rem(seq, 2), lax.rem(lax.div(seq, 2), 4)


def swap(array, mask, chan_mask=0):
    seqs, chans = lax.axis_size("seq"), lax.axis_size("chan")
    pairs = [(s * chans + c, (s ^ mask) * chans + (c ^ chan_mask)) for s in range(seqs) for c in range(chans)]
    return lax.ppermute(array, ("seq", "chan"), pairs)


def shift(array, steps=1):
    seqs, chans = lax.axis_size("seq"), lax.axis_size("chan")
    pairs = [(s * chans + c, s * chans + (c + steps) % chans) for s in range(seqs) for c in range(chans)]
    return lax.ppermute(array, ("seq", "chan"), pairs)


def in_order(found):
    chans, chan = lax.axis_size("chan"), lax.axis_index("chan")
    found = jnp.stack(found)
    return jnp.stack(
        [lax.dynamic_index_in_dim(found, lax.rem(chan + chans - c, chans), 0, False) for c in range(chans)]
    )


def gather_frame(held):
    mask = 1
    while mask < lax.axis_size("seq"):
        held = jnp.concatenate([held, swap(held, mask)], 0)
        mask *= 2
    return held


def thirds(values):
    parts = []
    for _ in range(3):
        part = lax.reduce_precision(values, 8, 7)
        parts.append(part.astype(jnp.bfloat16))
        values = values - part
    return parts


def spread(own, small, finish, early):
    units = own.shape[0]
    cut, third = units // 2, (units - early) // 3
    mid, end = early + third, early + 2 * third
    x, y, across = NEAR // 2, FAR // 2, (NEAR | FAR) // 2
    settle = lax.optimization_barrier
    pieces = []

    def add(array, *parts, behind=None):
        twin = swap(array if behind is None else settle((array, behind))[0], CORE)
        pieces.extend([(0, parts, array), (1, parts, twin)])
        return twin

    held_1, small_1 = settle((shift(own), shift(small)))
    held_2, small_2 = shift(held_1), shift(small_1)
    near_1, far_1 = swap(held_1, NEAR), swap(held_1, FAR)
    twin = add(held_1, (0, 1, 0, units))
    held_2, small_2, near_1, far_1, twin = settle((held_2, small_2, near_1, far_1, twin))
    held_3, small_3 = shift(held_2), shift(small_2)
    near_2 = swap(jnp.concatenate([held_2, far_1[:cut]], 0), NEAR)
    far_2 = swap(jnp.concatenate([held_2, near_1[cut:]], 0), FAR)
    twins = [
        add(near_1, (x, 1, 0, units)), add(far_1, (y, 1, 0, units)), add(held_2, (0, 2, 0, units)),
    ]
    held_3, small_3, near_2, far_2, twins = settle((held_3, small_3, near_2, far_2, twins))
    across_2 = shift(jnp.concatenate([near_2[units:], far_2[units:]], 0))
    near_3, far_3, first_3 = swap(held_3, NEAR), swap(held_3, FAR), swap(held_3[:early], NEAR | FAR)
    twins = add(near_2, (x, 2, 0, units), (across, 1, 0, cut))
    twins = add(far_2, (y, 2, 0, units), (across, 1, cut, units - cut), behind=twins)
    twins = add(held_3, (0, 3, 0, units), behind=twins)
    across_2, near_3, far_3, first_3, twins, extra = settle(
        (across_2, near_3, far_3, first_3, twins, finish(in_order([small, small_1, small_2, small_3])))
    )
    add(near_3, (x, 3, 0, units))
    add(far_3, (y, 3, 0, units))
    add(across_2, (across, 2, 0, units))
    add(first_3, (across, 3, 0, early))
    late = [
        (swap(far_3[early:mid], NEAR), (across, 3, early, third)),
        (swap(near_3[mid:end], FAR), (across, 3, mid, third)),
        (shift(across_2[end:]), (across, 3, end, units - end)),
    ]

    def last(gate):
        for array, part in late:
            add(settle((array, gate))[0], part)
        return pieces

    return pieces, last, extra


def groups_of(low, high, per_early, per_late):
    found = []
    for begin, per_chip, at in ((0, per_early, 0), (4 * per_early, per_late, per_early)):
        for chip in range(4):
            first = begin + chip * per_chip
            lowest, highest = max(first, low), min(first + per_chip, high)
            if lowest < highest:
                found.append((chip, at + lowest - first, lowest, highest - lowest))
    return tuple(found)


def own_slice(units, first, count, core):
    rows = units.shape[1] // 2
    return lax.dynamic_slice(units, (first, core * rows, 0), (count, rows, units.shape[2]))


def load_weights(groups, metas, chans, own, pieces, weights, sems):
    core, chip = place()
    chan = lax.axis_index("chan")
    base = groups[0][2]
    depth = own[0][0].shape[1]
    half = depth // 2

    def start_own(group, unit, units):
        at = pl.multiple_of(chan * depth, 16)
        for ref, begin in own:
            first, end = max(unit, begin), min(unit + units, begin + ref.shape[0])
            if first < end:
                dst = weights.at[pl.ds(first - base, end - first), pl.ds(at, depth), :]
                src = ref.at[pl.ds(first - begin, end - first)]
                pltpu.make_async_copy(src, dst, sems.at[group, 0]).start()

    def start_others(group, place_in, unit, units, chip_mask):
        for (core_mask, parts), ref in zip(metas, pieces):
            at = 0
            for mask, step, first, count in parts:
                low, high = max(first, place_in), min(first + count, place_in + units)
                if mask == chip_mask and low < high:
                    shard = lax.rem(chan + chans - step, chans)
                    row = pl.multiple_of(shard * depth + (core ^ core_mask) * half, 16)
                    to = unit - base + low - place_in
                    dst = weights.at[pl.ds(to, high - low), pl.ds(row, half), :]
                    src = ref.at[pl.ds(at + low - first, high - low)]
                    pltpu.make_async_copy(src, dst, sems.at[group, 2 * step - 1 + core_mask]).start()
                at += count

    def start(group):
        owner, place_in, unit, units = groups[group]
        start_own(group, unit, units)
        for here in range(4):

            @pl.when(chip == here)
            def _():
                start_others(group, place_in, unit, units, here ^ owner)

    for group in range(min(AHEAD, len(groups))):
        start(group)

    left = list(enumerate(groups))

    def need(end):
        while left and left[0][1][2] < end:
            group, (_, _, unit, units) = left.pop(0)
            taken = sum(
                max(0, min(unit + units, begin + ref.shape[0]) - max(unit, begin)) for ref, begin in own
            )
            mine = weights.at[pl.ds(unit - base, taken), pl.ds(0, depth), :]
            pltpu.make_async_copy(mine, mine, sems.at[group, 0]).wait()
            slice_of = weights.at[pl.ds(unit - base, units), pl.ds(0, half), :]
            for i in range(1, 2 * chans - 1):
                pltpu.make_async_copy(slice_of, slice_of, sems.at[group, i]).wait()
            if group + AHEAD < len(groups):
                start(group + AHEAD)

    return need


def inside(rows, width, first_row, first_col, height):
    row = first_row + lax.broadcasted_iota(jnp.int32, (rows, width, 1), 0)
    col = first_col + lax.broadcasted_iota(jnp.int32, (rows, width, 1), 1)
    ok = (row >= 0) & (row < height) & (col >= 0) & (col < LAT_W)
    return jnp.where(ok, 1.0, 0.0).astype(jnp.float32).reshape(rows * width, 1)


def norm_act(values, half_gain, half_shift, mask):
    mean_sq = jnp.mean(values * values, axis=1, keepdims=True)
    half = (values * lax.rsqrt(mean_sq + EPS) * half_gain + half_shift) * mask
    return half + half * jnp.tanh(half)


def set_rows(cols, values, low, width, rows):
    cells, chans = values.shape
    values = values.astype(jnp.bfloat16)
    high = low + cells // width
    for tap in range(3):
        first, end = max(low + 1 - tap, 0), min(high + 1 - tap, rows)
        skip = first - (low + 1 - tap)
        part = values[skip * width : (skip + end - first) * width]
        cols[first * width : end * width, tap * chans : (tap + 1) * chans] = part


def conv(cols, weights, unit, row, rows, width):
    chans = weights.shape[1]
    taps = [
        jnp.concatenate([weights[unit + tap + 3 * i] for i in range(3)], 0)
        for tap in range(3)
    ]
    window = cols[row * width : (row + rows) * width, :]
    every = jnp.dot(window, jnp.concatenate(taps, 1), preferred_element_type=jnp.float32)
    left, mid, right = (every[:, i * chans : (i + 1) * chans] for i in range(3))
    return pltpu.roll(left, 1, 0) + mid + pltpu.roll(right, rows * width - 1, 0)


def chunks(low, high):
    count = max(1, (high - low) // CHUNK)
    cuts = [low + (high - low) * i // count for i in range(count + 1)]
    return list(zip(cuts[:-1], cuts[1:]))


def set_columns(cols, values):
    cells, chans = values.shape
    cols[:cells, :chans] = pltpu.roll(values, 1, 0).astype(jnp.bfloat16)
    cols[:cells, chans : 2 * chans] = values.astype(jnp.bfloat16)
    cols[:cells, 2 * chans :] = pltpu.roll(values, cells - 1, 0).astype(jnp.bfloat16)


def tile_corner(slab_rows, tile_cols, halo):
    return (
        lax.axis_index("seq") * slab_rows - halo,
        lax.axis_index("chan") * tile_cols - HALO,
    )


def enter_kernel(static, params, in_weight, frame, out_ref, slab, wide, in_cols, sems):
    chans, rows, width, slab_rows, height = static
    tile_cols = LAT_W // chans
    lat, tokens = frame.shape[1:]
    blocks = LAT_W // tokens
    first_row, first_col = tile_corner(slab_rows, tile_cols, HALO)
    fetches = []
    for row in range(rows + 2):
        held = (first_row + row >= 0) & (first_row + row < height)
        at = jnp.clip(first_row + row, 0, height - 1)
        owner = lax.div(at, slab_rows) ^ lax.axis_index("seq")
        start = (owner * slab_rows + lax.rem(at, slab_rows)) * blocks
        fetch = pltpu.make_async_copy(frame.at[pl.ds(start, blocks)], slab.at[row], sems.at[row])
        pl.when(held)(fetch.start)
        fetches.append((held, fetch))
    for held, fetch in fetches:
        pl.when(held)(fetch.wait)
    for row in range(rows + 2):
        for block in range(blocks):
            at = 2 * HALO + block * tokens
            wide[row, at : at + tokens, :] = slab[row, block].astype(jnp.float32).T
    left = pl.multiple_of(lax.axis_index("chan") * tile_cols + HALO, 8)
    region = wide[:, pl.ds(left, width), :].reshape((rows + 2) * width, lat)
    mask = inside(rows + 2, width, first_row, first_col, height)
    set_columns(in_cols, jnp.where(mask > 0.0, region, 0.0))
    total = params[3, 0][None]
    for row_tap in range(3):
        part = in_cols[row_tap * width : (row_tap + rows) * width, :]
        total = total + jnp.dot(part, in_weight[row_tap], preferred_element_type=jnp.float32)
    out_ref[...] = total.astype(jnp.bfloat16)


def tile_kernel(static, *refs):
    chans, layers, begin, end, width, rows, slab_rows, height, groups, metas = static
    upsamples = end == layers
    params, up_bias, entered, res_ref, up_ref = refs[:5]
    pieces = refs[5 : 5 + len(metas)]
    n_outs = chans if upsamples else 1
    outs = refs[5 + len(metas) : 5 + len(metas) + n_outs]
    weights, held, cols_a, cols_b, last, woven, sems = refs[5 + len(metas) + n_outs :]
    gain, shift_by, bias = 0.5 * params[0], 0.5 * params[1], params[2]
    tile_cols = LAT_W // chans
    n_res = res_ref.shape[0]
    need = load_weights(groups, metas, chans, ((res_ref, 0), (up_ref, n_res)), pieces, weights, sems)
    base = groups[0][2]
    corner = tile_corner(slab_rows, tile_cols, (rows - slab_rows) // 2)

    def norm(values, index, row, stop):
        mask = inside(stop - row, width, corner[0] + row, corner[1], height)
        return norm_act(values, gain[index][None], shift_by[index][None], mask)

    held[...] = entered[...].astype(jnp.float32)
    for low, high in chunks(0, rows):
        set_rows(cols_a, norm(held[low * width : high * width, :], 2 * begin, low, high), low, width, rows)
    for layer in range(begin, end):
        margin, unit = 2 * (layer - begin) + 1, 18 * layer
        need(unit + 9)
        for low, high in chunks(margin, rows - margin):
            middle = conv(cols_a, weights, unit - base, low, high - low, width) + bias[2 * layer][None]
            set_rows(cols_b, norm(middle, 2 * layer + 1, low, high), low, width, rows)
        need(unit + 18)
        for low, high in chunks(margin + 1, rows - margin - 1):
            branch = conv(cols_b, weights, unit + 9 - base, low, high - low, width) + bias[2 * layer + 1][None]
            cells = slice(low * width, high * width)
            out_cells = slice((low - margin - 1) * width, (high - margin - 1) * width)
            stream = (held[cells, :] + branch).astype(jnp.bfloat16)
            if layer < end - 1:
                held[cells, :] = stream.astype(jnp.float32)
                set_rows(cols_a, norm(held[cells, :], 2 * layer + 2, low, high), low, width, rows)
            elif upsamples:
                mask = inside(high - low, width, corner[0] + low, corner[1], height)
                last[out_cells, :] = (stream.astype(jnp.float32) * mask).astype(jnp.bfloat16)
            else:
                outs[0][out_cells, :] = stream
    need(n_res + up_ref.shape[0])
    if not upsamples:
        return
    framed = last[...]
    rows = framed.shape[0] // width
    n_out = up_bias.shape[1]
    products = []
    for pair in range(up_ref.shape[0]):
        both = jnp.dot(framed, weights[n_res - base + pair], preferred_element_type=jnp.float32)
        products += [both[:, :n_out], both[:, n_out:]]
    cells = rows * width
    even, odd = [], []
    for row_tap in range(3):
        left, mid, right = products[3 * row_tap : 3 * row_tap + 3]
        even.append(pltpu.roll(left, 1, 0) + mid + right)
        odd.append(left + mid + pltpu.roll(right, cells - 1, 0))
    share = n_out // chans
    chan = lax.axis_index("chan")
    for row in range(slab_rows):
        for low in range(2):
            for parity, parts in ((0, even), (1, odd)):
                total = up_bias[...]
                for row_tap in range(3):
                    at = (row + 1 + (low + row_tap - 1) // 2) * width + HALO
                    total = total + parts[row_tap][at : at + tile_cols]
                for tile in range(woven.shape[0]):
                    lanes = total[:, 128 * tile : 128 * tile + 128]
                    if lanes.shape[1] < 128:
                        blank = jnp.zeros((tile_cols, 128 - lanes.shape[1]), jnp.float32)
                        lanes = jnp.concatenate([lanes, blank], 1)
                    woven[tile, pl.ds(parity, tile_cols, 2), :] = lanes
            turned = jnp.concatenate([woven[tile].T for tile in range(woven.shape[0])], 0)
            for owner in range(chans):
                part = turned[owner * share : (owner + 1) * share].astype(jnp.bfloat16)
                for step in range(chans):

                    @pl.when(lax.rem(chan + step, chans) == owner)
                    def _():
                        outs[step][2 * row + low] = part


def body(
    latent, in_weight, in_bias, norm_gain, norm_shift, res_weight, res_bias, up_weight, up_bias
):
    seqs, chans = lax.axis_size("seq"), lax.axis_size("chan")
    layers, _, taps, depth, ch = res_weight.shape
    outs = up_weight.shape[2]
    tokens, lat = latent.shape
    slab_rows = tokens * chans // LAT_W
    height = slab_rows * seqs
    tile_cols = LAT_W // chans
    width = -(-(tile_cols + 2 * HALO) // 16) * 16
    rows = slab_rows + 2 * (HALO - 1)
    vmem = pl.BlockSpec(memory_space=pltpu.VMEM)

    norms = [a.reshape(2 * layers, depth) for a in (norm_gain, norm_shift, res_bias)]
    ends = jnp.zeros((2 * layers, depth), jnp.float32)
    ends = ends.at[0].set(in_bias).at[1, : outs // chans].set(up_bias)
    smalls = [*thirds(jnp.concatenate(norms + [ends], 1)), in_weight.reshape(-1, ch)]
    smalls = jnp.concatenate(smalls, 0)
    n_small = smalls.shape[0]
    smalls = [smalls[:, at : at + tokens] for at in range(0, ch, tokens)]
    smalls = jnp.concatenate([*smalls, gather_frame(latent.T[None]).reshape(-1, tokens)], 0)

    def small_args(packed):
        n_lanes = ch // tokens
        frame = packed[:, n_small * n_lanes :].reshape(chans, seqs, lat, tokens).transpose(1, 0, 2, 3)
        frame = frame.reshape(seqs * chans, lat, tokens)
        packed = jnp.concatenate([packed[:, n_small * i : n_small * (i + 1)] for i in range(n_lanes)], 2)
        params = sum(packed[:, 2 * layers * i : 2 * layers * (i + 1)].astype(jnp.float32) for i in range(3))
        params = params.reshape(chans, 2 * layers, 4, depth).transpose(2, 1, 0, 3)
        up_b = params[3, 1, :, : outs // chans].reshape(1, outs)
        params = params.reshape(4, 2 * layers, ch)
        in_w = packed[:, 6 * layers :].reshape(chans, 3, taps // 3, lat // chans, ch)
        in_w = in_w.transpose(1, 2, 0, 3, 4).reshape(3, taps // 3 * lat, ch)
        entered = pl.pallas_call(
            functools.partial(enter_kernel, (chans, rows, width, slab_rows, height)),
            out_shape=jax.ShapeDtypeStruct((rows * width, ch), jnp.bfloat16),
            in_specs=[vmem, vmem, pl.BlockSpec(memory_space=pl.ANY)],
            out_specs=vmem,
            scratch_shapes=[
                pltpu.VMEM((rows + 2, LAT_W // tokens, lat, tokens), jnp.bfloat16),
                pltpu.VMEM((rows + 2, LAT_W + 4 * HALO, lat), jnp.float32),
                pltpu.VMEM(((rows + 2) * width, 3 * lat), jnp.bfloat16),
                pltpu.SemaphoreType.DMA((rows + 2,)),
            ],
            compiler_params=pltpu.CompilerParams(vmem_limit_bytes=ENTER_VMEM),
        )(params, in_w, frame)
        return params, up_b, entered

    res_units = res_weight.reshape(layers * 2 * taps, depth, ch)
    up_units = jnp.pad(up_weight, ((0, 1), (0, 0), (0, 0))).reshape(-1, 2, depth, outs)
    up_units = up_units.transpose(0, 2, 1, 3).reshape(-1, depth, 2 * outs)
    n_units = res_units.shape[0] + up_units.shape[0]
    per_early = -(-2 * taps // 4)
    per_late = -(-(n_units - 4 * per_early) // 4)
    begin = 4 * per_early + 3 * per_late
    tail = jnp.concatenate([res_units[begin:], up_units], 0)
    tail = jnp.pad(tail, ((0, per_late - tail.shape[0]), (0, 0), (0, 0)))
    core, chip = place()
    mine = [
        own_slice(res_units, chip * per_early, per_early, core),
        jnp.where(
            chip == 3,
            own_slice(tail, 0, per_late, core),
            own_slice(res_units, 4 * per_early + jnp.minimum(chip, 2) * per_late, per_late, core),
        ),
    ]
    pieces, last_pieces, small = spread(jnp.concatenate(mine, 0), smalls, small_args, per_early)
    params, up_b, stream = small

    def run(begin, end, rows, stream, pieces):
        first, stop = 2 * taps * begin, 2 * taps * end
        if end == layers:
            stop = 4 * (per_early + per_late)
            out_shape, n_out = (2 * slab_rows, outs // chans, 2 * tile_cols), chans
        else:
            out_shape, n_out = ((rows - 4 * (end - begin)) * width, ch), 1
        groups = groups_of(first, stop, per_early, per_late)
        metas = tuple((core, parts) for core, parts, _ in pieces)
        in_vmem = [params, up_b, stream]
        in_any = [res_units, up_units] + [array for _, _, array in pieces]
        cells = sum(rows - 2 * i for i in range(1, 2 * (end - begin) + 1)) * width
        return pl.pallas_call(
            functools.partial(
                tile_kernel, (chans, layers, begin, end, width, rows, slab_rows, height, groups, metas)
            ),
            out_shape=[jax.ShapeDtypeStruct(out_shape, jnp.bfloat16)] * n_out,
            in_specs=[vmem] * len(in_vmem) + [pl.BlockSpec(memory_space=pl.ANY)] * len(in_any),
            out_specs=[vmem] * n_out,
            scratch_shapes=[
                pltpu.VMEM((stop - first, ch, ch), jnp.bfloat16),
                pltpu.VMEM((rows * width, ch), jnp.float32),
                pltpu.VMEM((rows * width, 3 * ch), jnp.bfloat16),
                pltpu.VMEM((rows * width, 3 * ch), jnp.bfloat16),
                pltpu.VMEM(((slab_rows + 2) * width, ch), jnp.bfloat16),
                pltpu.VMEM((-(-outs // 128), 2 * tile_cols, 128), jnp.float32),
                pltpu.SemaphoreType.DMA((len(groups), 2 * chans - 1)),
            ],
            compiler_params=pltpu.CompilerParams(vmem_limit_bytes=VMEM_BYTES),
            cost_estimate=pl.CostEstimate(
                flops=4 * taps * ch * ch * cells, bytes_accessed=(stop - first) * ch * ch * 2, transcendentals=0
            ),
        )(*in_vmem, *in_any)

    [stream] = run(0, 1, rows, stream, pieces)
    shares = run(1, layers, rows - 4, stream, last_pieces(stream))
    shares = in_order([shares[0]] + [shift(shares[step], step) for step in range(1, chans)])
    return shares.transpose(2, 1, 0, 3).reshape(outs // chans, 2 * slab_rows, 2 * LAT_W)


def solution(mesh):
    placed = (
        P(("seq", "chan"), None),
        P(None, "chan", None),
        P("chan"),
        P(None, None, "chan"),
        P(None, None, "chan"),
        P(None, None, None, "chan", None),
        P(None, None, "chan"),
        P(None, "chan", None),
        P("chan"),
    )
    return jax.shard_map(
        body, mesh=mesh, in_specs=placed, out_specs=P("chan", "seq", None), check_vma=False
    )
```

```python
import functools
import jax
import jax.numpy as jnp
from jax import lax
from jax.experimental import pallas as pl
from jax.experimental.pallas import tpu as pltpu
from jax.sharding import PartitionSpec as P

LAT_W = 256
EPS = 1e-06
HALO = 8
CHUNK = 2
AHEAD = 2
VMEM_BYTES = 60 * 1024 * 1024
ENTER_VMEM = 16 * 1024 * 1024

CORE, NEAR, FAR = 1, 2, 4


def place():
    seq = lax.axis_index("seq")
    return lax.rem(seq, 2), lax.rem(lax.div(seq, 2), 4)


def swap(array, mask, chan_mask=0):
    seqs, chans = lax.axis_size("seq"), lax.axis_size("chan")
    pairs = [(s * chans + c, (s ^ mask) * chans + (c ^ chan_mask)) for s in range(seqs) for c in range(chans)]
    return lax.ppermute(array, ("seq", "chan"), pairs)


def shift(array, steps=1):
    seqs, chans = lax.axis_size("seq"), lax.axis_size("chan")
    pairs = [(s * chans + c, s * chans + (c + steps) % chans) for s in range(seqs) for c in range(chans)]
    return lax.ppermute(array, ("seq", "chan"), pairs)


def in_order(found):
    chans, chan = lax.axis_size("chan"), lax.axis_index("chan")
    found = jnp.stack(found)
    return jnp.stack(
        [lax.dynamic_index_in_dim(found, lax.rem(chan + chans - c, chans), 0, False) for c in range(chans)]
    )


def gather_frame(held):
    mask = 1
    while mask < lax.axis_size("seq"):
        held = jnp.concatenate([held, swap(held, mask)], 0)
        mask *= 2
    return held


def thirds(values):
    parts = []
    for _ in range(3):
        part = lax.reduce_precision(values, 8, 7)
        parts.append(part.astype(jnp.bfloat16))
        values = values - part
    return parts


def spread(own, small, finish, early, beside):
    units = own.shape[0]
    cut, third = units // 2, (units - early) // 3
    mid, end = early + third, early + 2 * third
    x, y, across = NEAR // 2, FAR // 2, (NEAR | FAR) // 2
    settle = lax.optimization_barrier
    pieces = []

    def add(array, *parts, behind=None):
        twin = swap(array if behind is None else settle((array, behind))[0], CORE)
        pieces.extend([(0, parts, array), (1, parts, twin)])
        return twin

    held_1, small_1 = settle((shift(own), shift(small)))
    held_2, small_2 = shift(held_1), shift(small_1)
    near_1, far_1 = swap(held_1, NEAR), swap(held_1, FAR)
    twin = add(held_1, (0, 1, 0, units))
    held_2, small_2, near_1, far_1, twin, beside = settle((held_2, small_2, near_1, far_1, twin, beside))
    held_3, small_3 = shift(held_2), shift(small_2)
    near_2 = swap(jnp.concatenate([held_2, far_1[:cut]], 0), NEAR)
    far_2 = swap(jnp.concatenate([held_2, near_1[cut:]], 0), FAR)
    twins = [
        add(near_1, (x, 1, 0, units)), add(far_1, (y, 1, 0, units)), add(held_2, (0, 2, 0, units)),
    ]
    held_3, small_3, near_2, far_2, twins = settle((held_3, small_3, near_2, far_2, twins))
    across_2 = shift(jnp.concatenate([near_2[units:], far_2[units:]], 0))
    near_3, far_3, first_3 = swap(held_3, NEAR), swap(held_3, FAR), swap(held_3[:early], NEAR | FAR)
    twins = add(near_2, (x, 2, 0, units), (across, 1, 0, cut))
    twins = add(far_2, (y, 2, 0, units), (across, 1, cut, units - cut), behind=twins)
    twins = add(held_3, (0, 3, 0, units), behind=twins)
    across_2, near_3, far_3, first_3, twins, extra = settle(
        (across_2, near_3, far_3, first_3, twins, finish(in_order([small, small_1, small_2, small_3])))
    )
    add(near_3, (x, 3, 0, units))
    add(far_3, (y, 3, 0, units))
    add(across_2, (across, 2, 0, units))
    add(first_3, (across, 3, 0, early))
    late = [
        (swap(far_3[early:mid], NEAR), (across, 3, early, third)),
        (swap(near_3[mid:end], FAR), (across, 3, mid, third)),
        (shift(across_2[end:]), (across, 3, end, units - end)),
    ]

    def last(gate):
        for array, part in late:
            add(settle((array, gate))[0], part)
        return pieces

    return pieces, last, extra, beside


def groups_of(low, high, per_early, per_late):
    found = []
    for begin, per_chip, at in ((0, per_early, 0), (4 * per_early, per_late, per_early)):
        for chip in range(4):
            first = begin + chip * per_chip
            lowest, highest = max(first, low), min(first + per_chip, high)
            if lowest < highest:
                found.append((chip, at + lowest - first, lowest, highest - lowest))
    return tuple(found)


def own_slice(units, first, count, core):
    rows = units.shape[1] // 2
    return lax.dynamic_slice(units, (first, core * rows, 0), (count, rows, units.shape[2]))


def load_weights(groups, metas, chans, own, pieces, weights, sems):
    core, chip = place()
    chan = lax.axis_index("chan")
    base = groups[0][2]
    depth = own[0][0].shape[1]
    half = depth // 2

    def start_own(group, unit, units):
        at = pl.multiple_of(chan * depth, 16)
        for ref, begin in own:
            first, end = max(unit, begin), min(unit + units, begin + ref.shape[0])
            if first < end:
                dst = weights.at[pl.ds(first - base, end - first), pl.ds(at, depth), :]
                src = ref.at[pl.ds(first - begin, end - first)]
                pltpu.make_async_copy(src, dst, sems.at[group, 0]).start()

    def start_others(group, place_in, unit, units, chip_mask):
        for (core_mask, parts), ref in zip(metas, pieces):
            at = 0
            for mask, step, first, count in parts:
                low, high = max(first, place_in), min(first + count, place_in + units)
                if mask == chip_mask and low < high:
                    shard = lax.rem(chan + chans - step, chans)
                    row = pl.multiple_of(shard * depth + (core ^ core_mask) * half, 16)
                    to = unit - base + low - place_in
                    dst = weights.at[pl.ds(to, high - low), pl.ds(row, half), :]
                    src = ref.at[pl.ds(at + low - first, high - low)]
                    pltpu.make_async_copy(src, dst, sems.at[group, 2 * step - 1 + core_mask]).start()
                at += count

    def start(group):
        owner, place_in, unit, units = groups[group]
        start_own(group, unit, units)
        for here in range(4):

            @pl.when(chip == here)
            def _():
                start_others(group, place_in, unit, units, here ^ owner)

    for group in range(min(AHEAD, len(groups))):
        start(group)

    left = list(enumerate(groups))

    def need(end):
        while left and left[0][1][2] < end:
            group, (_, _, unit, units) = left.pop(0)
            taken = sum(
                max(0, min(unit + units, begin + ref.shape[0]) - max(unit, begin)) for ref, begin in own
            )
            mine = weights.at[pl.ds(unit - base, taken), pl.ds(0, depth), :]
            pltpu.make_async_copy(mine, mine, sems.at[group, 0]).wait()
            slice_of = weights.at[pl.ds(unit - base, units), pl.ds(0, half), :]
            for i in range(1, 2 * chans - 1):
                pltpu.make_async_copy(slice_of, slice_of, sems.at[group, i]).wait()
            if group + AHEAD < len(groups):
                start(group + AHEAD)

    return need


def inside(rows, width, first_row, first_col, height):
    row = first_row + lax.broadcasted_iota(jnp.int32, (rows, width, 1), 0)
    col = first_col + lax.broadcasted_iota(jnp.int32, (rows, width, 1), 1)
    ok = (row >= 0) & (row < height) & (col >= 0) & (col < LAT_W)
    return jnp.where(ok, 1.0, 0.0).astype(jnp.float32).reshape(rows * width, 1)


def norm_act(values, half_gain, half_shift, mask):
    mean_sq = jnp.mean(values * values, axis=1, keepdims=True)
    half = (values * lax.rsqrt(mean_sq + EPS) * half_gain + half_shift) * mask
    return half + half * jnp.tanh(half)


def set_rows(cols, values, low, width, rows):
    cells, chans = values.shape
    values = values.astype(jnp.bfloat16)
    high = low + cells // width
    for tap in range(3):
        first, end = max(low + 1 - tap, 0), min(high + 1 - tap, rows)
        skip = first - (low + 1 - tap)
        part = values[skip * width : (skip + end - first) * width]
        cols[first * width : end * width, tap * chans : (tap + 1) * chans] = part


def conv(cols, weights, unit, row, rows, width):
    chans = weights.shape[1]
    taps = [
        jnp.concatenate([weights[unit + tap + 3 * i] for i in range(3)], 0)
        for tap in range(3)
    ]
    window = cols[row * width : (row + rows) * width, :]
    every = jnp.dot(window, jnp.concatenate(taps, 1), preferred_element_type=jnp.float32)
    left, mid, right = (every[:, i * chans : (i + 1) * chans] for i in range(3))
    return pltpu.roll(left, 1, 0) + mid + pltpu.roll(right, rows * width - 1, 0)


def chunks(low, high):
    count = max(1, (high - low) // CHUNK)
    cuts = [low + (high - low) * i // count for i in range(count + 1)]
    return list(zip(cuts[:-1], cuts[1:]))


def set_columns(cols, values):
    cells, chans = values.shape
    cols[:cells, :chans] = pltpu.roll(values, 1, 0).astype(jnp.bfloat16)
    cols[:cells, chans : 2 * chans] = values.astype(jnp.bfloat16)
    cols[:cells, 2 * chans :] = pltpu.roll(values, cells - 1, 0).astype(jnp.bfloat16)


def tile_corner(slab_rows, tile_cols, halo):
    return (
        lax.axis_index("seq") * slab_rows - halo,
        lax.axis_index("chan") * tile_cols - HALO,
    )


def enter_kernel(static, params, in_weight, frame, out_ref, slab, wide, in_cols, sems):
    chans, rows, width, slab_rows, height = static
    tile_cols = LAT_W // chans
    lat, tokens = frame.shape[1:]
    blocks = LAT_W // tokens
    first_row, first_col = tile_corner(slab_rows, tile_cols, HALO)
    fetches = []
    for row in range(rows + 2):
        held = (first_row + row >= 0) & (first_row + row < height)
        at = jnp.clip(first_row + row, 0, height - 1)
        owner = lax.div(at, slab_rows) ^ lax.axis_index("seq")
        start = (owner * slab_rows + lax.rem(at, slab_rows)) * blocks
        fetch = pltpu.make_async_copy(frame.at[pl.ds(start, blocks)], slab.at[row], sems.at[row])
        pl.when(held)(fetch.start)
        fetches.append((held, fetch))
    for held, fetch in fetches:
        pl.when(held)(fetch.wait)
    for row in range(rows + 2):
        for block in range(blocks):
            at = 2 * HALO + block * tokens
            wide[row, at : at + tokens, :] = slab[row, block].astype(jnp.float32).T
    left = pl.multiple_of(lax.axis_index("chan") * tile_cols + HALO, 8)
    region = wide[:, pl.ds(left, width), :].reshape((rows + 2) * width, lat)
    mask = inside(rows + 2, width, first_row, first_col, height)
    set_columns(in_cols, jnp.where(mask > 0.0, region, 0.0))
    total = params[3, 0][None]
    for row_tap in range(3):
        part = in_cols[row_tap * width : (row_tap + rows) * width, :]
        total = total + jnp.dot(part, in_weight[row_tap], preferred_element_type=jnp.float32)
    out_ref[...] = total.astype(jnp.bfloat16)


def tile_kernel(static, *refs):
    chans, layers, begin, end, width, rows, slab_rows, height, groups, metas = static
    upsamples = end == layers
    params, up_bias, entered, res_ref, up_ref = refs[:5]
    pieces = refs[5 : 5 + len(metas)]
    n_outs = chans if upsamples else 1
    outs = refs[5 + len(metas) : 5 + len(metas) + n_outs]
    weights, held, cols_a, cols_b, last, woven, sems = refs[5 + len(metas) + n_outs :]
    gain, shift_by, bias = 0.5 * params[0], 0.5 * params[1], params[2]
    tile_cols = LAT_W // chans
    n_res = res_ref.shape[0]
    need = load_weights(groups, metas, chans, ((res_ref, 0), (up_ref, n_res)), pieces, weights, sems)
    base = groups[0][2]
    corner = tile_corner(slab_rows, tile_cols, (rows - slab_rows) // 2)

    def norm(values, index, row, stop):
        mask = inside(stop - row, width, corner[0] + row, corner[1], height)
        return norm_act(values, gain[index][None], shift_by[index][None], mask)

    held[...] = entered[...].astype(jnp.float32)
    for low, high in chunks(0, rows):
        set_rows(cols_a, norm(held[low * width : high * width, :], 2 * begin, low, high), low, width, rows)
    for layer in range(begin, end):
        margin, unit = 2 * (layer - begin) + 1, 18 * layer
        need(unit + 9)
        for low, high in chunks(margin, rows - margin):
            middle = conv(cols_a, weights, unit - base, low, high - low, width) + bias[2 * layer][None]
            set_rows(cols_b, norm(middle, 2 * layer + 1, low, high), low, width, rows)
        need(unit + 18)
        for low, high in chunks(margin + 1, rows - margin - 1):
            branch = conv(cols_b, weights, unit + 9 - base, low, high - low, width) + bias[2 * layer + 1][None]
            cells = slice(low * width, high * width)
            out_cells = slice((low - margin - 1) * width, (high - margin - 1) * width)
            stream = (held[cells, :] + branch).astype(jnp.bfloat16)
            if layer < end - 1:
                held[cells, :] = stream.astype(jnp.float32)
                set_rows(cols_a, norm(held[cells, :], 2 * layer + 2, low, high), low, width, rows)
            elif upsamples:
                mask = inside(high - low, width, corner[0] + low, corner[1], height)
                last[out_cells, :] = (stream.astype(jnp.float32) * mask).astype(jnp.bfloat16)
            else:
                outs[0][out_cells, :] = stream
    need(n_res + up_ref.shape[0])
    if not upsamples:
        return
    framed = last[...]
    rows = framed.shape[0] // width
    n_out = up_bias.shape[1]
    products = []
    for pair in range(up_ref.shape[0]):
        both = jnp.dot(framed, weights[n_res - base + pair], preferred_element_type=jnp.float32)
        products += [both[:, :n_out], both[:, n_out:]]
    cells = rows * width
    even, odd = [], []
    for row_tap in range(3):
        left, mid, right = products[3 * row_tap : 3 * row_tap + 3]
        even.append(pltpu.roll(left, 1, 0) + mid + right)
        odd.append(left + mid + pltpu.roll(right, cells - 1, 0))
    share = n_out // chans
    chan = lax.axis_index("chan")
    for row in range(slab_rows):
        for low in range(2):
            for parity, parts in ((0, even), (1, odd)):
                total = up_bias[...]
                for row_tap in range(3):
                    at = (row + 1 + (low + row_tap - 1) // 2) * width + HALO
                    total = total + parts[row_tap][at : at + tile_cols]
                for tile in range(woven.shape[0]):
                    lanes = total[:, 128 * tile : 128 * tile + 128]
                    if lanes.shape[1] < 128:
                        blank = jnp.zeros((tile_cols, 128 - lanes.shape[1]), jnp.float32)
                        lanes = jnp.concatenate([lanes, blank], 1)
                    woven[tile, pl.ds(parity, tile_cols, 2), :] = lanes
            turned = jnp.concatenate([woven[tile].T for tile in range(woven.shape[0])], 0)
            for owner in range(chans):
                part = turned[owner * share : (owner + 1) * share].astype(jnp.bfloat16)
                for step in range(chans):

                    @pl.when(lax.rem(chan + step, chans) == owner)
                    def _():
                        outs[step][2 * row + low] = part


def body(
    latent, in_weight, in_bias, norm_gain, norm_shift, res_weight, res_bias, up_weight, up_bias
):
    seqs, chans = lax.axis_size("seq"), lax.axis_size("chan")
    layers, _, taps, depth, ch = res_weight.shape
    outs = up_weight.shape[2]
    tokens, lat = latent.shape
    slab_rows = tokens * chans // LAT_W
    height = slab_rows * seqs
    tile_cols = LAT_W // chans
    width = -(-(tile_cols + 2 * HALO) // 16) * 16
    rows = slab_rows + 2 * (HALO - 1)
    vmem = pl.BlockSpec(memory_space=pltpu.VMEM)

    ends = jnp.concatenate([in_bias, up_bias, jnp.zeros(2 * depth - in_bias.size - up_bias.size, jnp.float32)])
    ends = jnp.pad(ends.reshape(1, 2, depth), ((0, layers - 1), (0, 0), (0, 0)))
    norms = jnp.concatenate([norm_gain, norm_shift, res_bias, ends], 2).reshape(2 * layers, ch)
    smalls = [*thirds(norms), in_weight.reshape(-1, ch)]
    smalls = jnp.concatenate(smalls, 0)
    n_small = smalls.shape[0]
    smalls = [smalls[:, at : at + tokens] for at in range(0, ch, tokens)]
    smalls = jnp.concatenate([*smalls, gather_frame(latent.T[None]).reshape(-1, tokens)], 0)

    def small_args(packed):
        n_lanes = ch // tokens
        frame = packed[:, n_small * n_lanes :].reshape(chans, seqs, lat, tokens).transpose(1, 0, 2, 3)
        frame = frame.reshape(seqs * chans, lat, tokens)
        packed = jnp.concatenate([packed[:, n_small * i : n_small * (i + 1)] for i in range(n_lanes)], 2)
        params = sum(packed[:, 2 * layers * i : 2 * layers * (i + 1)].astype(jnp.float32) for i in range(3))
        params = params.reshape(chans, 2 * layers, 4, depth).transpose(2, 1, 0, 3)
        up_b = params[3, 1, :, : outs // chans].reshape(1, outs)
        params = params.reshape(4, 2 * layers, ch)
        in_w = packed[:, 6 * layers :].reshape(chans, 3, taps // 3, lat // chans, ch)
        in_w = in_w.transpose(1, 2, 0, 3, 4).reshape(3, taps // 3 * lat, ch)
        entered = pl.pallas_call(
            functools.partial(enter_kernel, (chans, rows, width, slab_rows, height)),
            out_shape=jax.ShapeDtypeStruct((rows * width, ch), jnp.bfloat16),
            in_specs=[vmem, vmem, pl.BlockSpec(memory_space=pl.ANY)],
            out_specs=vmem,
            scratch_shapes=[
                pltpu.VMEM((rows + 2, LAT_W // tokens, lat, tokens), jnp.bfloat16),
                pltpu.VMEM((rows + 2, LAT_W + 4 * HALO, lat), jnp.float32),
                pltpu.VMEM(((rows + 2) * width, 3 * lat), jnp.bfloat16),
                pltpu.SemaphoreType.DMA((rows + 2,)),
            ],
            compiler_params=pltpu.CompilerParams(vmem_limit_bytes=ENTER_VMEM),
        )(params, in_w, frame)
        return params, up_b, entered

    res_units = res_weight.reshape(layers * 2 * taps, depth, ch)
    up_units = jnp.pad(up_weight, ((0, 1), (0, 0), (0, 0))).reshape(-1, 2, depth, outs)
    up_units = up_units.transpose(0, 2, 1, 3).reshape(-1, depth, 2 * outs)
    n_units = res_units.shape[0] + up_units.shape[0]
    per_early = -(-2 * taps // 4)
    per_late = -(-(n_units - 4 * per_early) // 4)
    begin = 4 * per_early + 3 * per_late
    core, chip = place()
    half = own_slice(up_weight, 0, taps, core)
    odd = jnp.pad(half[1::2], ((0, taps % 2), (0, 0), (0, 0)))
    tail = [own_slice(res_units, begin, res_units.shape[0] - begin, core), jnp.concatenate([half[0::2], odd], 2)]
    tail.append(jnp.zeros((begin + per_late - n_units,) + tail[1].shape[1:], tail[1].dtype))
    mine = [
        own_slice(res_units, chip * per_early, per_early, core),
        jnp.where(
            chip == 3,
            jnp.concatenate(tail, 0),
            own_slice(res_units, 4 * per_early + jnp.minimum(chip, 2) * per_late, per_late, core),
        ),
    ]
    pieces, last_pieces, small, up_units = spread(
        jnp.concatenate(mine, 0), smalls, small_args, per_early, up_units
    )
    params, up_b, stream = small

    def run(begin, end, rows, stream, pieces):
        first, stop = 2 * taps * begin, 2 * taps * end
        if end == layers:
            stop = 4 * (per_early + per_late)
            out_shape, n_out = (2 * slab_rows, outs // chans, 2 * tile_cols), chans
        else:
            out_shape, n_out = ((rows - 4 * (end - begin)) * width, ch), 1
        groups = groups_of(first, stop, per_early, per_late)
        metas = tuple((core, parts) for core, parts, _ in pieces)
        in_vmem = [params, up_b, stream]
        in_any = [res_units, up_units] + [array for _, _, array in pieces]
        cells = sum(rows - 2 * i for i in range(1, 2 * (end - begin) + 1)) * width
        return pl.pallas_call(
            functools.partial(
                tile_kernel, (chans, layers, begin, end, width, rows, slab_rows, height, groups, metas)
            ),
            out_shape=[jax.ShapeDtypeStruct(out_shape, jnp.bfloat16)] * n_out,
            in_specs=[vmem] * len(in_vmem) + [pl.BlockSpec(memory_space=pl.ANY)] * len(in_any),
            out_specs=[vmem] * n_out,
            scratch_shapes=[
                pltpu.VMEM((stop - first, ch, ch), jnp.bfloat16),
                pltpu.VMEM((rows * width, ch), jnp.float32),
                pltpu.VMEM((rows * width, 3 * ch), jnp.bfloat16),
                pltpu.VMEM((rows * width, 3 * ch), jnp.bfloat16),
                pltpu.VMEM(((slab_rows + 2) * width, ch), jnp.bfloat16),
                pltpu.VMEM((-(-outs // 128), 2 * tile_cols, 128), jnp.float32),
                pltpu.SemaphoreType.DMA((len(groups), 2 * chans - 1)),
            ],
            compiler_params=pltpu.CompilerParams(vmem_limit_bytes=VMEM_BYTES),
            cost_estimate=pl.CostEstimate(
                flops=4 * taps * ch * ch * cells, bytes_accessed=(stop - first) * ch * ch * 2, transcendentals=0
            ),
        )(*in_vmem, *in_any)

    [stream] = run(0, 1, rows, stream, pieces)
    shares = run(1, layers, rows - 4, stream, last_pieces(stream))
    shares = in_order([shares[0]] + [shift(shares[step], step) for step in range(1, chans)])
    return shares.transpose(2, 1, 0, 3).reshape(outs // chans, 2 * slab_rows, 2 * LAT_W)


def solution(mesh):
    placed = (
        P(("seq", "chan"), None),
        P(None, "chan", None),
        P("chan"),
        P(None, None, "chan"),
        P(None, None, "chan"),
        P(None, None, None, "chan", None),
        P(None, None, "chan"),
        P(None, "chan", None),
        P("chan"),
    )
    return jax.shard_map(
        body, mesh=mesh, in_specs=placed, out_specs=P("chan", "seq", None), check_vma=False
    )
```

```python
import functools
import jax
import jax.numpy as jnp
from jax import lax
from jax.experimental import pallas as pl
from jax.experimental.pallas import tpu as pltpu
from jax.sharding import PartitionSpec as P

LAT_W = 256
EPS = 1e-06
HALO = 8
CHUNK = 2
AHEAD = 2
VMEM_BYTES = 60 * 1024 * 1024
ENTER_VMEM = 16 * 1024 * 1024

CORE, NEAR, FAR = 1, 2, 4


def place():
    seq = lax.axis_index("seq")
    return lax.rem(seq, 2), lax.rem(lax.div(seq, 2), 4)


def swap(array, mask, chan_mask=0):
    seqs, chans = lax.axis_size("seq"), lax.axis_size("chan")
    pairs = [(s * chans + c, (s ^ mask) * chans + (c ^ chan_mask)) for s in range(seqs) for c in range(chans)]
    return lax.ppermute(array, ("seq", "chan"), pairs)


def shift(array, steps=1):
    seqs, chans = lax.axis_size("seq"), lax.axis_size("chan")
    pairs = [(s * chans + c, s * chans + (c + steps) % chans) for s in range(seqs) for c in range(chans)]
    return lax.ppermute(array, ("seq", "chan"), pairs)


def in_order(found):
    chans, chan = lax.axis_size("chan"), lax.axis_index("chan")
    found = jnp.stack(found)
    return jnp.stack(
        [lax.dynamic_index_in_dim(found, lax.rem(chan + chans - c, chans), 0, False) for c in range(chans)]
    )


def gather_frame(held):
    mask = 1
    while mask < lax.axis_size("seq"):
        held = jnp.concatenate([held, swap(held, mask)], 0)
        mask *= 2
    return held


def thirds(values):
    parts = []
    for _ in range(3):
        part = lax.reduce_precision(values, 8, 7)
        parts.append(part.astype(jnp.bfloat16))
        values = values - part
    return parts


def spread(own, small, finish, early, beside):
    units = own.shape[0]
    cut, third = units // 2, (units - early) // 3
    mid, end = early + third, early + 2 * third
    x, y, across = NEAR // 2, FAR // 2, (NEAR | FAR) // 2
    settle = lax.optimization_barrier
    pieces = []

    def add(array, *parts, behind=None):
        twin = swap(array if behind is None else settle((array, behind))[0], CORE)
        pieces.extend([(0, parts, array), (1, parts, twin)])
        return twin

    held_1, small_1 = settle((shift(own), shift(small)))
    held_2, small_2 = shift(held_1), shift(small_1)
    near_1, far_1 = swap(held_1, NEAR), swap(held_1, FAR)
    twin = add(held_1, (0, 1, 0, units))
    held_2, small_2, near_1, far_1, twin, beside = settle((held_2, small_2, near_1, far_1, twin, beside))
    held_3, small_3 = shift(held_2), shift(small_2)
    near_2 = swap(jnp.concatenate([held_2, far_1[:cut]], 0), NEAR)
    far_2 = swap(jnp.concatenate([held_2, near_1[cut:]], 0), FAR)
    twins = [
        add(near_1, (x, 1, 0, units)), add(far_1, (y, 1, 0, units)), add(held_2, (0, 2, 0, units)),
    ]
    held_3, small_3, near_2, far_2, twins = settle((held_3, small_3, near_2, far_2, twins))
    across_2 = shift(jnp.concatenate([near_2[units:], far_2[units:]], 0))
    near_3, far_3, first_3 = swap(held_3, NEAR), swap(held_3, FAR), swap(held_3[:early], NEAR | FAR)
    twins = add(near_2, (x, 2, 0, units), (across, 1, 0, cut))
    twins = add(far_2, (y, 2, 0, units), (across, 1, cut, units - cut), behind=twins)
    twins = add(held_3, (0, 3, 0, units), behind=twins)
    across_2, near_3, far_3, first_3, twins, extra = settle(
        (across_2, near_3, far_3, first_3, twins, finish(in_order([small, small_1, small_2, small_3])))
    )
    add(near_3, (x, 3, 0, units))
    add(far_3, (y, 3, 0, units))
    add(across_2, (across, 2, 0, units))
    add(first_3, (across, 3, 0, early))
    late = [
        (swap(far_3[early:mid], NEAR), (across, 3, early, third)),
        (swap(near_3[mid:end], FAR), (across, 3, mid, third)),
        (shift(across_2[end:]), (across, 3, end, units - end)),
    ]

    def last(gate):
        for array, part in late:
            add(settle((array, gate))[0], part)
        return pieces

    return pieces, last, extra, beside


def groups_of(low, high, per_early, per_late):
    found = []
    for begin, per_chip, at in ((0, per_early, 0), (4 * per_early, per_late, per_early)):
        for chip in range(4):
            first = begin + chip * per_chip
            lowest, highest = max(first, low), min(first + per_chip, high)
            if lowest < highest:
                found.append((chip, at + lowest - first, lowest, highest - lowest))
    return tuple(found)


def own_slice(units, first, count, core):
    rows = units.shape[1] // 2
    return lax.dynamic_slice(units, (first, core * rows, 0), (count, rows, units.shape[2]))


def load_weights(groups, metas, chans, own, pieces, weights, sems):
    core, chip = place()
    chan = lax.axis_index("chan")
    base = groups[0][2]
    depth = own[0][0].shape[1]
    half = depth // 2

    def start_own(group, unit, units):
        at = pl.multiple_of(chan * depth, 16)
        for ref, begin in own:
            first, end = max(unit, begin), min(unit + units, begin + ref.shape[0])
            if first < end:
                dst = weights.at[pl.ds(first - base, end - first), pl.ds(at, depth), :]
                src = ref.at[pl.ds(first - begin, end - first)]
                pltpu.make_async_copy(src, dst, sems.at[group, 0]).start()

    def start_others(group, place_in, unit, units, chip_mask):
        for (core_mask, parts), ref in zip(metas, pieces):
            at = 0
            for mask, step, first, count in parts:
                low, high = max(first, place_in), min(first + count, place_in + units)
                if mask == chip_mask and low < high:
                    shard = lax.rem(chan + chans - step, chans)
                    row = pl.multiple_of(shard * depth + (core ^ core_mask) * half, 16)
                    to = unit - base + low - place_in
                    dst = weights.at[pl.ds(to, high - low), pl.ds(row, half), :]
                    src = ref.at[pl.ds(at + low - first, high - low)]
                    pltpu.make_async_copy(src, dst, sems.at[group, 2 * step - 1 + core_mask]).start()
                at += count

    def start(group):
        owner, place_in, unit, units = groups[group]
        start_own(group, unit, units)
        for here in range(4):

            @pl.when(chip == here)
            def _():
                start_others(group, place_in, unit, units, here ^ owner)

    for group in range(min(AHEAD, len(groups))):
        start(group)

    left = list(enumerate(groups))

    def need(end):
        while left and left[0][1][2] < end:
            group, (_, _, unit, units) = left.pop(0)
            taken = sum(
                max(0, min(unit + units, begin + ref.shape[0]) - max(unit, begin)) for ref, begin in own
            )
            mine = weights.at[pl.ds(unit - base, taken), pl.ds(0, depth), :]
            pltpu.make_async_copy(mine, mine, sems.at[group, 0]).wait()
            slice_of = weights.at[pl.ds(unit - base, units), pl.ds(0, half), :]
            for i in range(1, 2 * chans - 1):
                pltpu.make_async_copy(slice_of, slice_of, sems.at[group, i]).wait()
            if group + AHEAD < len(groups):
                start(group + AHEAD)

    return need


def inside(rows, width, first_row, first_col, height):
    row = first_row + lax.broadcasted_iota(jnp.int32, (rows, width, 1), 0)
    col = first_col + lax.broadcasted_iota(jnp.int32, (rows, width, 1), 1)
    ok = (row >= 0) & (row < height) & (col >= 0) & (col < LAT_W)
    return jnp.where(ok, 1.0, 0.0).astype(jnp.float32).reshape(rows * width, 1)


def norm_act(values, half_gain, half_shift, mask):
    mean_sq = jnp.mean(values * values, axis=1, keepdims=True)
    half = (values * lax.rsqrt(mean_sq + EPS) * half_gain + half_shift) * mask
    return half + half * jnp.tanh(half)


def set_rows(cols, values, low, width, rows):
    cells, chans = values.shape
    values = values.astype(jnp.bfloat16)
    high = low + cells // width
    for tap in range(3):
        first, end = max(low + 1 - tap, 0), min(high + 1 - tap, rows)
        skip = first - (low + 1 - tap)
        part = values[skip * width : (skip + end - first) * width]
        cols[first * width : end * width, tap * chans : (tap + 1) * chans] = part


def conv(cols, weights, unit, row, rows, width):
    chans = weights.shape[1]
    taps = [
        jnp.concatenate([weights[unit + tap + 3 * i] for i in range(3)], 0)
        for tap in range(3)
    ]
    window = cols[row * width : (row + rows) * width, :]
    every = jnp.dot(window, jnp.concatenate(taps, 1), preferred_element_type=jnp.float32)
    left, mid, right = (every[:, i * chans : (i + 1) * chans] for i in range(3))
    return pltpu.roll(left, 1, 0) + mid + pltpu.roll(right, rows * width - 1, 0)


def chunks(low, high):
    count = max(1, (high - low) // CHUNK)
    cuts = [low + (high - low) * i // count for i in range(count + 1)]
    return list(zip(cuts[:-1], cuts[1:]))


def set_columns(cols, values):
    cells, chans = values.shape
    cols[:cells, :chans] = pltpu.roll(values, 1, 0).astype(jnp.bfloat16)
    cols[:cells, chans : 2 * chans] = values.astype(jnp.bfloat16)
    cols[:cells, 2 * chans :] = pltpu.roll(values, cells - 1, 0).astype(jnp.bfloat16)


def tile_corner(slab_rows, tile_cols, halo):
    return (
        lax.axis_index("seq") * slab_rows - halo,
        lax.axis_index("chan") * tile_cols - HALO,
    )


def enter_kernel(static, params, in_weight, frame, out_ref, slab, wide, in_cols, sems):
    chans, rows, width, slab_rows, height = static
    tile_cols = LAT_W // chans
    lat, tokens = frame.shape[1:]
    blocks = LAT_W // tokens
    first_row, first_col = tile_corner(slab_rows, tile_cols, HALO)
    fetches = []
    for row in range(rows + 2):
        held = (first_row + row >= 0) & (first_row + row < height)
        at = jnp.clip(first_row + row, 0, height - 1)
        owner = lax.div(at, slab_rows) ^ lax.axis_index("seq")
        start = (owner * slab_rows + lax.rem(at, slab_rows)) * blocks
        fetch = pltpu.make_async_copy(frame.at[pl.ds(start, blocks)], slab.at[row], sems.at[row])
        pl.when(held)(fetch.start)
        fetches.append((held, fetch))
    for held, fetch in fetches:
        pl.when(held)(fetch.wait)
    for row in range(rows + 2):
        for block in range(blocks):
            at = 2 * HALO + block * tokens
            wide[row, at : at + tokens, :] = slab[row, block].astype(jnp.float32).T
    left = pl.multiple_of(lax.axis_index("chan") * tile_cols + HALO, 8)
    region = wide[:, pl.ds(left, width), :].reshape((rows + 2) * width, lat)
    mask = inside(rows + 2, width, first_row, first_col, height)
    set_columns(in_cols, jnp.where(mask > 0.0, region, 0.0))
    total = params[3, 0][None]
    for row_tap in range(3):
        part = in_cols[row_tap * width : (row_tap + rows) * width, :]
        total = total + jnp.dot(part, in_weight[row_tap], preferred_element_type=jnp.float32)
    out_ref[...] = total.astype(jnp.bfloat16)


def tile_kernel(static, *refs):
    chans, layers, begin, end, width, rows, slab_rows, height, groups, metas = static
    upsamples = end == layers
    params, up_bias, entered, res_ref, up_ref = refs[:5]
    pieces = refs[5 : 5 + len(metas)]
    n_outs = chans if upsamples else 1
    outs = refs[5 + len(metas) : 5 + len(metas) + n_outs]
    weights, held, cols_a, cols_b, last, woven, shares, sems = refs[5 + len(metas) + n_outs :]
    gain, shift_by, bias = 0.5 * params[0], 0.5 * params[1], params[2]
    tile_cols = LAT_W // chans
    n_res = res_ref.shape[0]
    need = load_weights(groups, metas, chans, ((res_ref, 0), (up_ref, n_res)), pieces, weights, sems)
    base = groups[0][2]
    corner = tile_corner(slab_rows, tile_cols, (rows - slab_rows) // 2)

    def norm(values, index, row, stop):
        mask = inside(stop - row, width, corner[0] + row, corner[1], height)
        return norm_act(values, gain[index][None], shift_by[index][None], mask)

    held[...] = entered[...].astype(jnp.float32)
    for low, high in chunks(0, rows):
        set_rows(cols_a, norm(held[low * width : high * width, :], 2 * begin, low, high), low, width, rows)
    for layer in range(begin, end):
        margin, unit = 2 * (layer - begin) + 1, 18 * layer
        need(unit + 9)
        for low, high in chunks(margin, rows - margin):
            middle = conv(cols_a, weights, unit - base, low, high - low, width) + bias[2 * layer][None]
            set_rows(cols_b, norm(middle, 2 * layer + 1, low, high), low, width, rows)
        need(unit + 18)
        for low, high in chunks(margin + 1, rows - margin - 1):
            branch = conv(cols_b, weights, unit + 9 - base, low, high - low, width) + bias[2 * layer + 1][None]
            cells = slice(low * width, high * width)
            out_cells = slice((low - margin - 1) * width, (high - margin - 1) * width)
            stream = (held[cells, :] + branch).astype(jnp.bfloat16)
            if layer < end - 1:
                held[cells, :] = stream.astype(jnp.float32)
                set_rows(cols_a, norm(held[cells, :], 2 * layer + 2, low, high), low, width, rows)
            elif upsamples:
                mask = inside(high - low, width, corner[0] + low, corner[1], height)
                last[out_cells, :] = (stream.astype(jnp.float32) * mask).astype(jnp.bfloat16)
            else:
                outs[0][out_cells, :] = stream
    need(n_res + up_ref.shape[0])
    if not upsamples:
        return
    framed = last[...]
    rows = framed.shape[0] // width
    n_out = up_bias.shape[1]
    products = []
    for pair in range(up_ref.shape[0]):
        both = jnp.dot(framed, weights[n_res - base + pair], preferred_element_type=jnp.float32)
        products += [both[:, :n_out], both[:, n_out:]]
    cells = rows * width
    even, odd = [], []
    for row_tap in range(3):
        left, mid, right = products[3 * row_tap : 3 * row_tap + 3]
        even.append(pltpu.roll(left, 1, 0) + mid + right)
        odd.append(left + mid + pltpu.roll(right, cells - 1, 0))
    share = n_out // chans
    chan = lax.axis_index("chan")
    for row in range(slab_rows):
        for low in range(2):
            for parity, parts in ((0, even), (1, odd)):
                total = up_bias[...]
                for row_tap in range(3):
                    at = (row + 1 + (low + row_tap - 1) // 2) * width + HALO
                    total = total + parts[row_tap][at : at + tile_cols]
                for tile in range(woven.shape[0]):
                    lanes = total[:, 128 * tile : 128 * tile + 128]
                    if lanes.shape[1] < 128:
                        blank = jnp.zeros((tile_cols, 128 - lanes.shape[1]), jnp.float32)
                        lanes = jnp.concatenate([lanes, blank], 1)
                    woven[tile, pl.ds(parity, tile_cols, 2), :] = lanes
            turned = jnp.concatenate([woven[tile].T for tile in range(woven.shape[0])], 0)
            for owner in range(chans):
                part = turned[owner * share : (owner + 1) * share].astype(jnp.bfloat16)
                shares[owner, 2 * row + low] = part
    for step in range(chans):
        outs[step][...] = shares[lax.rem(chan + step, chans)]


def body(
    latent, in_weight, in_bias, norm_gain, norm_shift, res_weight, res_bias, up_weight, up_bias
):
    seqs, chans = lax.axis_size("seq"), lax.axis_size("chan")
    layers, _, taps, depth, ch = res_weight.shape
    outs = up_weight.shape[2]
    tokens, lat = latent.shape
    slab_rows = tokens * chans // LAT_W
    height = slab_rows * seqs
    tile_cols = LAT_W // chans
    width = -(-(tile_cols + 2 * HALO) // 16) * 16
    rows = slab_rows + 2 * (HALO - 1)
    vmem = pl.BlockSpec(memory_space=pltpu.VMEM)

    ends = jnp.concatenate([in_bias, up_bias, jnp.zeros(2 * depth - in_bias.size - up_bias.size, jnp.float32)])
    ends = jnp.pad(ends.reshape(1, 2, depth), ((0, layers - 1), (0, 0), (0, 0)))
    norms = jnp.concatenate([norm_gain, norm_shift, res_bias, ends], 2).reshape(2 * layers, ch)
    smalls = [*thirds(norms), in_weight.reshape(-1, ch)]
    smalls = jnp.concatenate(smalls, 0)
    n_small = smalls.shape[0]
    smalls = [smalls[:, at : at + tokens] for at in range(0, ch, tokens)]
    smalls = jnp.concatenate([*smalls, gather_frame(latent.T[None]).reshape(-1, tokens)], 0)

    def small_args(packed):
        n_lanes = ch // tokens
        frame = packed[:, n_small * n_lanes :].reshape(chans, seqs, lat, tokens).transpose(1, 0, 2, 3)
        frame = frame.reshape(seqs * chans, lat, tokens)
        packed = jnp.concatenate([packed[:, n_small * i : n_small * (i + 1)] for i in range(n_lanes)], 2)
        params = sum(packed[:, 2 * layers * i : 2 * layers * (i + 1)].astype(jnp.float32) for i in range(3))
        params = params.reshape(chans, 2 * layers, 4, depth).transpose(2, 1, 0, 3)
        up_b = params[3, 1, :, : outs // chans].reshape(1, outs)
        params = params.reshape(4, 2 * layers, ch)
        in_w = packed[:, 6 * layers :].reshape(chans, 3, taps // 3, lat // chans, ch)
        in_w = in_w.transpose(1, 2, 0, 3, 4).reshape(3, taps // 3 * lat, ch)
        entered = pl.pallas_call(
            functools.partial(enter_kernel, (chans, rows, width, slab_rows, height)),
            out_shape=jax.ShapeDtypeStruct((rows * width, ch), jnp.bfloat16),
            in_specs=[vmem, vmem, pl.BlockSpec(memory_space=pl.ANY)],
            out_specs=vmem,
            scratch_shapes=[
                pltpu.VMEM((rows + 2, LAT_W // tokens, lat, tokens), jnp.bfloat16),
                pltpu.VMEM((rows + 2, LAT_W + 4 * HALO, lat), jnp.float32),
                pltpu.VMEM(((rows + 2) * width, 3 * lat), jnp.bfloat16),
                pltpu.SemaphoreType.DMA((rows + 2,)),
            ],
            compiler_params=pltpu.CompilerParams(vmem_limit_bytes=ENTER_VMEM),
        )(params, in_w, frame)
        return params, up_b, entered

    res_units = res_weight.reshape(layers * 2 * taps, depth, ch)
    up_units = jnp.pad(up_weight, ((0, 1), (0, 0), (0, 0))).reshape(-1, 2, depth, outs)
    up_units = up_units.transpose(0, 2, 1, 3).reshape(-1, depth, 2 * outs)
    n_units = res_units.shape[0] + up_units.shape[0]
    per_early = -(-2 * taps // 4)
    per_late = -(-(n_units - 4 * per_early) // 4)
    begin = 4 * per_early + 3 * per_late
    core, chip = place()
    half = own_slice(up_weight, 0, taps, core)
    odd = jnp.pad(half[1::2], ((0, taps % 2), (0, 0), (0, 0)))
    tail = [own_slice(res_units, begin, res_units.shape[0] - begin, core), jnp.concatenate([half[0::2], odd], 2)]
    tail.append(jnp.zeros((begin + per_late - n_units,) + tail[1].shape[1:], tail[1].dtype))
    mine = [
        own_slice(res_units, chip * per_early, per_early, core),
        jnp.where(
            chip == 3,
            jnp.concatenate(tail, 0),
            own_slice(res_units, 4 * per_early + jnp.minimum(chip, 2) * per_late, per_late, core),
        ),
    ]
    pieces, last_pieces, small, up_units = spread(
        jnp.concatenate(mine, 0), smalls, small_args, per_early, up_units
    )
    params, up_b, stream = small

    def run(begin, end, rows, stream, pieces):
        first, stop = 2 * taps * begin, 2 * taps * end
        if end == layers:
            stop = 4 * (per_early + per_late)
            out_shape, n_out = (2 * slab_rows, outs // chans, 2 * tile_cols), chans
        else:
            out_shape, n_out = ((rows - 4 * (end - begin)) * width, ch), 1
        groups = groups_of(first, stop, per_early, per_late)
        metas = tuple((core, parts) for core, parts, _ in pieces)
        in_vmem = [params, up_b, stream]
        in_any = [res_units, up_units] + [array for _, _, array in pieces]
        cells = sum(rows - 2 * i for i in range(1, 2 * (end - begin) + 1)) * width
        return pl.pallas_call(
            functools.partial(
                tile_kernel, (chans, layers, begin, end, width, rows, slab_rows, height, groups, metas)
            ),
            out_shape=[jax.ShapeDtypeStruct(out_shape, jnp.bfloat16)] * n_out,
            in_specs=[vmem] * len(in_vmem) + [pl.BlockSpec(memory_space=pl.ANY)] * len(in_any),
            out_specs=[vmem] * n_out,
            scratch_shapes=[
                pltpu.VMEM((stop - first, ch, ch), jnp.bfloat16),
                pltpu.VMEM((rows * width, ch), jnp.float32),
                pltpu.VMEM((rows * width, 3 * ch), jnp.bfloat16),
                pltpu.VMEM((rows * width, 3 * ch), jnp.bfloat16),
                pltpu.VMEM(((slab_rows + 2) * width, ch), jnp.bfloat16),
                pltpu.VMEM((-(-outs // 128), 2 * tile_cols, 128), jnp.float32),
                pltpu.VMEM((chans, 2 * slab_rows, outs // chans, 2 * tile_cols), jnp.bfloat16),
                pltpu.SemaphoreType.DMA((len(groups), 2 * chans - 1)),
            ],
            compiler_params=pltpu.CompilerParams(vmem_limit_bytes=VMEM_BYTES),
            cost_estimate=pl.CostEstimate(
                flops=4 * taps * ch * ch * cells, bytes_accessed=(stop - first) * ch * ch * 2, transcendentals=0
            ),
        )(*in_vmem, *in_any)

    [stream] = run(0, 1, rows, stream, pieces)
    shares = run(1, layers, rows - 4, stream, last_pieces(stream))
    shares = in_order([shares[0]] + [shift(shares[step], step) for step in range(1, chans)])
    return shares.transpose(2, 1, 0, 3).reshape(outs // chans, 2 * slab_rows, 2 * LAT_W)


def solution(mesh):
    placed = (
        P(("seq", "chan"), None),
        P(None, "chan", None),
        P("chan"),
        P(None, None, "chan"),
        P(None, None, "chan"),
        P(None, None, None, "chan", None),
        P(None, None, "chan"),
        P(None, "chan", None),
        P("chan"),
    )
    return jax.shard_map(
        body, mesh=mesh, in_specs=placed, out_specs=P("chan", "seq", None), check_vma=False
    )
```
